32 devices in a mesh: shard: 4 (over x, core), context: 2 (over y), tensor: 4 (over z).
Axes of the slice: x: 2, y: 2, z: 4, core: 2. Of those that a mesh axis runs over, the one named last changes fastest.
Arguments:
- tokens: bfloat16 [4, 1152, 2048], P('shard', ('context', 'tensor')), may hold values from -6 to 6
- cotangent: bfloat16 [4, 1152, 2048], P('shard', ('context', 'tensor')), may hold values from -6 to 6
- segments: int32 [4, 1152], P('shard'), may hold values from 0 to 4, as said below
- first_gain: bfloat16 [2048], P('shard'), may hold values from 0.099609375 to 1.8984375
- second_gain: bfloat16 [2048], P('shard'), may hold values from 0.099609375 to 1.8984375
- query_weight: bfloat16 [2048, 2048], P('shard', 'tensor'), may hold values from -0.25 to 0.25
- key_weight: bfloat16 [2048, 512], P('shard', 'tensor'), may hold values from -0.125 to 0.125
- value_weight: bfloat16 [2048, 512], P('shard', 'tensor'), may hold values from -0.125 to 0.125
- output_weight: bfloat16 [2048, 2048], P('shard', 'tensor'), may hold values from -1 to 1
- gate_weight: bfloat16 [2048, 8192], P('shard', 'tensor'), may hold values from -0.125 to 0.125
- up_matrix: bfloat16 [2048, 8192], P('shard', 'tensor'), may hold values from -0.125 to 0.125
- down_weight: bfloat16 [2048, 8192], P('shard', 'tensor'), may hold values from -0.125 to 0.125
Outputs:
- layer_output: bfloat16 [4, 1152, 2048], P('shard', ('context', 'tensor'))
- tokens_grad: bfloat16 [4, 1152, 2048], P('shard', ('context', 'tensor'))
- first_gain_grad: float32 [2048], P('shard')
- second_gain_grad: float32 [2048], P('shard')
- query_weight_grad: float32 [2048, 2048], P('shard', 'tensor')
- key_weight_grad: float32 [2048, 512], P('shard', 'tensor')
- value_weight_grad: float32 [2048, 512], P('shard', 'tensor')
- output_weight_grad: float32 [2048, 2048], P('shard', 'tensor')
- gate_weight_grad: float32 [2048, 8192], P('shard', 'tensor')
- up_weight_grad: float32 [2048, 8192], P('shard', 'tensor')
- down_weight_grad: float32 [2048, 8192], P('shard', 'tensor')
The draws below stay inside these ranges and needn't reach their ends.
Inputs may be any that keep to these rules, and one draw needn't show every extreme that they name: segments[b, i] counts the document starts among positions 1 to i of sequence b (several may share a position), so it never falls along a sequence, is 0 at position 0 and 4 at the last position; no document starts after position 287 and before position 865.
All inputs are finite; a program needn't handle non-finite values.
Results may differ from the reference program's by a relative error of at most 0.025.
Values may be sent and summed in bfloat16 or wider, within the bound.
No kernel may reach another device: no remote copies, remote signals or barrier semaphores. Data moves between devices by JAX's collectives and lax.ppermute only.
A program may use at most 256 MiB of HBM per device.

```python
import jax
import jax.numpy as jnp
from jax import lax

D = 2048
H = 32
KV = 8
HD = 64
FF = 8192
SEQ_LEN = 1152
CUTS = 4
NSEQ = 4


def draw_segments(key, part):
    key = jax.random.fold_in(key, 11)
    early_key, late_key = jax.random.split(key)
    early = jax.random.randint(early_key, (NSEQ, CUTS // 2), 1, SEQ_LEN // 4)
    late = jax.random.randint(late_key, (NSEQ, CUTS - CUTS // 2), 3 * SEQ_LEN // 4 + 1, SEQ_LEN)
    cut_points = jnp.concatenate([early, late], axis=1)
    index_row = jnp.arange(SEQ_LEN, dtype=jnp.int32)
    counted = (index_row[None, :, None] >= cut_points[:, None, :]).astype(jnp.int32)
    return jnp.sum(counted, axis=2).astype(jnp.int32)


def spiked(values, stream_key, source, target, parts, factor):
    owner, partner = [(jnp.arange(values.shape[position]) // (values.shape[position] // parts)).reshape([-1 if axis == position else 1 for axis in range(values.ndim)]) for position in (source, target)]
    chosen = jax.random.permutation(stream_key, parts)[partner]
    strong = (owner == chosen) | (owner == (partner + parts // 2) % parts)
    return jnp.where(strong, factor * values, values)


def block_scale(rng, dims, shards, smallest, top_value):
    level, own = 1.0, jax.random.fold_in(rng, 6)
    for axis_at, blocks in shards:
        steps = jnp.exp(jax.random.uniform(jax.random.fold_in(own, axis_at), (blocks,), jnp.float32, smallest / len(shards), top_value / len(shards)))
        level = level * jnp.repeat(steps, dims[axis_at] // blocks).reshape([-1 if axis == axis_at else 1 for axis in range(len(dims))])
    return level


def centred(stream_key, shape, scale, bound, cuts=(), kind=jnp.bfloat16):
    drawn = scale * jax.random.normal(stream_key, shape, jnp.float32)
    if cuts:
        drawn = drawn * block_scale(stream_key, shape, cuts, -0.22, 0.18)
    return jnp.clip(drawn, -bound, bound).astype(kind)


def noise_with(key, extent, spread, most, cuts, heavy, kind=jnp.bfloat16):
    array = spread * jax.random.normal(key, extent, jnp.float32)
    if cuts:
        array = array * block_scale(key, extent, cuts, -0.22, 0.18)
    return jnp.clip(spiked(array, jax.random.fold_in(key, 3), *heavy), -most, most).astype(kind)


def setup_inputs(seed: int = 0) -> dict:
    arg_keys = jax.random.split(jax.random.key(seed), 13)
    return {
        "tokens": noise_with(arg_keys[0], (NSEQ, SEQ_LEN, D), 1.0, 6.0, ((0, 4), (1, 8)), (0, 2, 4, 2.0)),
        "cotangent": noise_with(arg_keys[1], (NSEQ, SEQ_LEN, D), 1.0, 6.0, ((0, 4), (1, 8)), (0, 2, 4, 2.0)),
        "segments": draw_segments(jax.random.fold_in(arg_keys[12], 71), 0),
        "first_gain": jnp.clip(1.0 + 0.18 * jax.random.normal(arg_keys[3], (D,), jnp.float32), 0.099609375, 1.8984375).astype(jnp.bfloat16),
        "second_gain": jnp.clip(1.0 + 0.18 * jax.random.normal(arg_keys[4], (D,), jnp.float32), 0.099609375, 1.8984375).astype(jnp.bfloat16),
        "query_weight": centred(arg_keys[5], (D, H * HD), (D // 4) ** -0.5, 0.25, ((0, 4), (1, 4))),
        "key_weight": centred(arg_keys[6], (D, KV * HD), D ** -0.5, 0.125, ((0, 4), (1, 4))),
        "value_weight": centred(arg_keys[7], (D, KV * HD), D ** -0.5, 0.125, ((0, 4), (1, 4))),
        "output_weight": centred(arg_keys[8], (D, H * HD), (H * HD // 64) ** -0.5, 1.0, ((0, 4), (1, 4))),
        "gate_weight": centred(arg_keys[9], (D, FF), D ** -0.5, 0.125, ((0, 4), (1, 4))),
        "up_matrix": centred(arg_keys[10], (D, FF), D ** -0.5, 0.125, ((0, 4), (1, 4))),
        "down_weight": centred(arg_keys[11], (D, FF), (FF // 4) ** -0.5, 0.125, ((0, 4), (1, 4))),
    }


EPS = 1e-05
THETA = 500000.0
MASKED = -1e+30

@jax.custom_vjp
def low(v):
    return lax.optimization_barrier(v.astype(jnp.bfloat16)).astype(jnp.float32)

@jax.custom_vjp
def low_back(v):
    return v

def low_keep(v):
    return (low(v), None)

def low_pass(kept, grad):
    return (grad,)

def back_keep(v):
    return (v, None)

def back_low(kept, grad):
    return (low(grad),)
low.defvjp(low_keep, low_pass)
low_back.defvjp(back_keep, back_low)

def positions_of(segments):
    index_row = jnp.arange(segments.shape[1], dtype=jnp.int32)
    changed = jnp.concatenate([jnp.ones((segments.shape[0], 1), bool), segments[:, 1:] != segments[:, :-1]], axis=1)
    starts = lax.cummax(jnp.where(changed, index_row[None, :], 0).astype(jnp.int32), axis=1)
    return (index_row[None, :] - starts).astype(jnp.int32)

def rope_tables(positions):
    freq_index = jnp.arange(HD // 2, dtype=jnp.float32)
    inverse = THETA ** (-2.0 * freq_index / HD)
    angles = positions.astype(jnp.float32)[:, None] * inverse[None, :]
    cosines = jnp.cos(angles)
    sines = jnp.sin(angles)
    return (jnp.concatenate([cosines, cosines], axis=-1), jnp.concatenate([sines, sines], axis=-1))

def rotate(values, cosines, sines):
    middle = values.shape[-1] // 2
    turned = jnp.concatenate([-values[..., middle:], values[..., :middle]], axis=-1)
    return values * cosines + turned * sines

def rms_scale(values):
    return lax.rsqrt(lax.optimization_barrier(jnp.mean(values * values, axis=-1, keepdims=True)) + EPS)

def project(rows, weight):
    return jnp.einsum('bld,dc->blc', rows, weight, precision=lax.Precision.HIGHEST)

def project_back(rows, weight):
    return jnp.einsum('blc,dc->bld', rows, weight, precision=lax.Precision.HIGHEST)

def attend(items):
    query_seq, key_seq, value_seq, seg_row, pos_row = items
    seq_len = query_seq.shape[0]
    cosines, sines = rope_tables(pos_row)
    query_rot = low(rotate(query_seq, cosines[:, None, None, :], sines[:, None, None, :]))
    key_rot = low(rotate(key_seq, cosines[:, None, :], sines[:, None, :]))
    scores = low_back(jnp.einsum('lkga,mka->kglm', query_rot, key_rot, precision=lax.Precision.HIGHEST) * HD ** (-0.5))
    index_row = jnp.arange(seq_len, dtype=jnp.int32)
    allowed = (seg_row[:, None] == seg_row[None, :]) & (index_row[None, :] <= index_row[:, None])
    scores = jnp.where(allowed, scores, MASKED)
    probs = low(jax.nn.softmax(scores, axis=-1))
    attended = jnp.einsum('kglm,mka->lkga', probs, value_seq, precision=lax.Precision.HIGHEST)
    return low_back(low(attended))

def reference(tokens, cotangent, segments, first_gain, second_gain, query_weight, key_weight, value_weight, output_weight, gate_weight, up_matrix, down_weight):
    positions = positions_of(segments)

    def forward(input_rows, gain_one, gain_two, w_query, w_key, w_value, w_output, w_gate, w_up, w_down):
        nseq_count, seq_len = (input_rows.shape[0], input_rows.shape[1])
        group = H // KV
        normed_one = low(input_rows * rms_scale(input_rows) * gain_one)
        query_all = low_back(low(project(normed_one, w_query)))
        key_all = low_back(low(project(normed_one, w_key)))
        value_all = low_back(low(project(normed_one, w_value)))
        attended = lax.map(jax.checkpoint(attend), (query_all.reshape(nseq_count, seq_len, KV, group, HD), key_all.reshape(nseq_count, seq_len, KV, HD), value_all.reshape(nseq_count, seq_len, KV, HD), segments, positions))
        attn_out = low_back(project_back(attended.reshape(nseq_count, seq_len, H * HD), w_output))
        hidden_one = input_rows + attn_out
        normed_two = low(hidden_one * rms_scale(hidden_one) * gain_two)
        gate_all = low_back(project(normed_two, w_gate))
        up_all = low_back(project(normed_two, w_up))
        hidden_mid = low(jax.nn.silu(gate_all) * up_all)
        ffn_out = low_back(project_back(hidden_mid, w_down))
        return hidden_one + ffn_out
    primals = (tokens.astype(jnp.float32), first_gain.astype(jnp.float32), second_gain.astype(jnp.float32), query_weight.astype(jnp.float32), key_weight.astype(jnp.float32), value_weight.astype(jnp.float32), output_weight.astype(jnp.float32), gate_weight.astype(jnp.float32), up_matrix.astype(jnp.float32), down_weight.astype(jnp.float32))
    result, pullback = jax.vjp(forward, *primals)
    grads = pullback(cotangent.astype(jnp.float32))
    return (result.astype(jnp.bfloat16), grads[0].astype(jnp.bfloat16), grads[1], grads[2], grads[3], grads[4], grads[5], grads[6], grads[7], grads[8], grads[9])
```

```python
import functools

import jax
import jax.numpy as jnp
from jax import lax
from jax.experimental import pallas as pl
from jax.experimental.pallas import tpu as pltpu
from jax.sharding import PartitionSpec as P

H = 32
KV = 8
HD = 64
GROUP = H // KV
QW = GROUP * HD
PW = QW + 2 * HD

EPS = 1e-05
THETA = 500000.0
MASKED = -1e30
BF = jnp.bfloat16
F32 = jnp.float32


def mm(a, b, dims, out=F32):
    return lax.dot_general(a, b, (dims, ((), ())), preferred_element_type=F32).astype(out)


def shift(values, step):
    return lax.ppermute(values, "tensor", [(i, (i + step) % 4) for i in range(4)])


def flip(values):
    return lax.ppermute(values, "context", [(0, 1), (1, 0)])


def xor_send(values, bit, count):
    return lax.ppermute(values, "shard", [(i, i ^ bit) for i in range(count)])


def shard_bits(count):
    bits = []
    bit = count // 2
    while bit:
        bits.append(bit)
        bit //= 2
    return bits


def xor_order(count):
    order = [0]
    for bit in shard_bits(count):
        order = order + [o | bit for o in order]
    return order


class Order:
    def __init__(self):
        self.mark = jnp.zeros((), F32)

    def after(self, values):
        values, _ = lax.optimization_barrier((values, self.mark))
        return values

    def wait(self, values):
        values, self.mark = lax.optimization_barrier((values, self.mark))
        return values


def add_bf(a, b):
    return (a.astype(F32) + b.astype(F32)).astype(BF)


def reduce_rest(kept, bits, count):
    for bit in bits:
        half = kept.shape[0] // 2
        kept = add_bf(kept[:half], xor_send(kept[half:], bit, count))
    return kept


def split_at(rows):
    return -(-rows // 32) * 16


def gather_rows_start(rows):
    return shift(rows, 1), shift(rows, -1)


def gather_rows_next(near):
    right, left = near
    mid = split_at(left.shape[0])
    return shift(left[:mid], -1), shift(right[mid:], 1)


def gather_rows_end(rows, near, far):
    return jnp.concatenate([rows, near[1], far[0], far[1], near[0]], axis=0)


def sum_rows_start(terms):
    length = terms.shape[0] // 4
    mid = split_at(length)
    far = terms[2 * length : 3 * length]
    return shift(far[:mid], 1), shift(far[mid:], -1)


def sum_rows_next(terms, far):
    length = terms.shape[0] // 4
    mid = split_at(length)
    t1, t3 = terms[length : 2 * length], terms[3 * length :]
    t1 = jnp.concatenate([add_bf(t1[:mid], far[0]), t1[mid:]], axis=0)
    t3 = jnp.concatenate([t3[:mid], add_bf(t3[mid:], far[1])], axis=0)
    return shift(t1, 1), shift(t3, -1)


def sum_rows_end(terms, near):
    own = terms[: terms.shape[0] // 4]
    return own.astype(F32) + near[0].astype(F32) + near[1].astype(F32)


def pick_turn(values):
    lane = lax.broadcasted_iota(jnp.int32, values.shape, 1)
    ahead = pltpu.roll(values, 2 * HD - HD // 2, 1)
    behind = pltpu.roll(values, HD // 2, 1)
    return jnp.where(lane % HD < HD // 2, ahead, behind)


def slot_of(block, z, length):
    return pl.multiple_of(((block - z + 4) % 4) * length, 16)


def causal_width(block, length, total):
    return min(total, -(-((block + 1) * length) // 128) * 128)


def masked_scores(q, k, start, first_row):
    s = mm(q, k, ((1,), (1,)))
    col = lax.broadcasted_iota(jnp.int32, s.shape, 1)
    row = lax.broadcasted_iota(jnp.int32, s.shape, 0) + first_row
    return jnp.where((col <= row) & (col >= start), s, MASKED)


def attn_forward_kernel(meta, own, oth, start, cos, sin, att_own, att_oth, rot, lse, nat):
    y, z = meta[0], meta[1]
    total = rot.shape[0]
    half = total // 2
    length = half // 4
    for src, base in ((own, y * half), (oth, (1 - y) * half)):
        for b in range(4):
            at = pl.ds(pl.multiple_of(base + b * length, 16), length)
            rows = src[pl.ds(slot_of(b, z, length), length), :].astype(BF)
            c, s = cos[at, :], sin[at, :]
            for part in range(PW // 128):
                u = rows[:, part * 128 : (part + 1) * 128].astype(F32)
                turned = u * c + pick_turn(u) * s
                if part == PW // 128 - 1:
                    lane = lax.broadcasted_iota(jnp.int32, u.shape, 1)
                    turned = jnp.where(lane < HD, turned, u)
                rot[at, part * 128 : (part + 1) * 128] = turned.astype(BF).astype(F32)
    for b in range(8):
        at = slice(b * length, (b + 1) * length)
        width = causal_width(b, length, total)
        k = rot[:width, QW : QW + HD].astype(BF)
        v = rot[:width, QW + HD :].astype(BF)
        heads = []
        for h in range(GROUP):
            q = (rot[at, h * HD : (h + 1) * HD] * HD**-0.5).astype(BF)
            s = masked_scores(q, k, start[at, :], b * length)
            top = jnp.max(s, axis=1, keepdims=True)
            p = jnp.exp(s - top)
            norm = jnp.sum(p, axis=1, keepdims=True)
            lse[at, h : h + 1] = top + jnp.log(norm)
            p = (p * (1.0 / norm)).astype(BF)
            heads.append(mm(p, v, ((1,), (0,))))
        nat[at, :] = jnp.concatenate(heads, axis=1)
    for dst, base in ((att_own, y * half), (att_oth, (1 - y) * half)):
        for b in range(4):
            at = pl.ds(pl.multiple_of(base + b * length, 16), length)
            dst[pl.ds(slot_of(b, z, length), length), :] = nat[at, :]


def attn_backward_kernel(
    meta, rot, lse, own, oth, start, cos, sin, d_own, d_oth, nat, d_nat, dk, dv
):
    y, z = meta[0], meta[1]
    total = rot.shape[0]
    half = total // 2
    length = half // 4
    for src, base in ((own, y * half), (oth, (1 - y) * half)):
        for b in range(4):
            at = pl.ds(pl.multiple_of(base + b * length, 16), length)
            nat[at, :] = src[pl.ds(slot_of(b, z, length), length), :]
    dk[...] = jnp.zeros_like(dk)
    dv[...] = jnp.zeros_like(dv)
    for b in range(8):
        at = slice(b * length, (b + 1) * length)
        width = causal_width(b, length, total)
        k = rot[:width, QW : QW + HD].astype(BF)
        v = rot[:width, QW + HD :].astype(BF)
        d_heads = []
        for h in range(GROUP):
            q = (rot[at, h * HD : (h + 1) * HD] * HD**-0.5).astype(BF)
            g = nat[at, h * HD : (h + 1) * HD].astype(BF)
            p = jnp.exp(masked_scores(q, k, start[at, :], b * length) - lse[at, h : h + 1])
            dp = mm(g, v, ((1,), (1,)))
            delta = jnp.sum(p * dp, axis=1, keepdims=True)
            ds = (p * (dp - delta)).astype(BF)
            d_heads.append(mm(ds, k, ((1,), (0,))) * HD**-0.5)
            dk[:width, :] += mm(ds, q, ((0,), (0,)))
            dv[:width, :] += mm(p.astype(BF), g, ((0,), (0,)))
        d_q = jnp.concatenate(d_heads, axis=1)
        for part in range(QW // 128):
            u = d_q[:, part * 128 : (part + 1) * 128]
            u = u * cos[at, :] - pick_turn(u) * sin[at, :]
            d_nat[at, part * 128 : (part + 1) * 128] = u
    for b in range(8):
        at = slice(b * length, (b + 1) * length)
        u = jnp.concatenate([dk[at, :], dv[at, :]], axis=1)
        turned = u * cos[at, :] - pick_turn(u) * sin[at, :]
        lane = lax.broadcasted_iota(jnp.int32, u.shape, 1)
        d_nat[at, QW:] = jnp.where(lane < HD, turned, u)
    for dst, base in ((d_own, y * half), (d_oth, (1 - y) * half)):
        for b in range(4):
            at = pl.ds(pl.multiple_of(base + b * length, 16), length)
            dst[pl.ds(slot_of(b, z, length), length), :] = d_nat[at, :]


VMEM = pl.BlockSpec(memory_space=pltpu.VMEM)
SMEM = pl.BlockSpec(memory_space=pltpu.SMEM)
ATTN_PARAMS = dict(vmem_limit_bytes=24 * 1024 * 1024)


def attn_forward(meta, own, oth, start, cos, sin):
    half = own.shape[0]
    return pl.pallas_call(
        attn_forward_kernel,
        out_shape=(
            jax.ShapeDtypeStruct((half, QW), F32),
            jax.ShapeDtypeStruct((half, QW), F32),
            jax.ShapeDtypeStruct((2 * half, PW), F32),
            jax.ShapeDtypeStruct((2 * half, GROUP), F32),
        ),
        in_specs=[SMEM] + [VMEM] * 5,
        out_specs=[VMEM] * 4,
        scratch_shapes=[pltpu.VMEM((2 * half, QW), F32)],
        compiler_params=pltpu.CompilerParams(**ATTN_PARAMS),
        cost_estimate=pl.CostEstimate(
            flops=8 * half * half * QW, bytes_accessed=8 * half * PW, transcendentals=8 * half * half
        ),
        name="attend_forward",
    )(meta, own, oth, start, cos, sin)


def attn_backward(meta, rot, lse, own, oth, start, cos, sin):
    half = own.shape[0]
    return pl.pallas_call(
        attn_backward_kernel,
        out_shape=(
            jax.ShapeDtypeStruct((half, PW), F32),
            jax.ShapeDtypeStruct((half, PW), F32),
        ),
        in_specs=[SMEM] + [VMEM] * 7,
        out_specs=[VMEM] * 2,
        scratch_shapes=[
            pltpu.VMEM((2 * half, QW), F32),
            pltpu.VMEM((2 * half, PW), F32),
            pltpu.VMEM((2 * half, HD), F32),
            pltpu.VMEM((2 * half, HD), F32),
        ],
        compiler_params=pltpu.CompilerParams(**ATTN_PARAMS),
        cost_estimate=pl.CostEstimate(
            flops=20 * half * half * QW, bytes_accessed=12 * half * PW, transcendentals=8 * half * half
        ),
        name="attend_backward",
    )(meta, rot, lse, own, oth, start, cos, sin)


def positions_of(seg_row):
    index_row = jnp.arange(seg_row.shape[0], dtype=jnp.int32)
    changed = jnp.concatenate([jnp.ones((1,), bool), seg_row[1:] != seg_row[:-1]])
    starts = lax.cummax(jnp.where(changed, index_row, 0), axis=0)
    return index_row - starts, starts


def rope_tables(positions):
    freq_index = jnp.arange(HD // 2, dtype=F32)
    inverse = THETA ** (-2.0 * freq_index / HD)
    angles = positions.astype(F32)[:, None] * inverse[None, :]
    cosines = jnp.cos(angles)
    sines = jnp.sin(angles)
    return (
        jnp.concatenate([cosines] * 4, axis=-1),
        jnp.concatenate([-sines, sines] * 2, axis=-1),
    )


def rms_scale(values):
    return lax.rsqrt(jnp.mean(values * values, axis=-1, keepdims=True) + EPS)


def norm_backward(grad_normed, normalized, scales, gain):
    rescaled = grad_normed * gain
    grad_input = scales * (
        rescaled - normalized * jnp.mean(rescaled * normalized, axis=-1, keepdims=True)
    )
    return grad_input


def shards(
    count,
    tokens,
    cotangent,
    segments,
    first_gain,
    second_gain,
    query_weight,
    key_weight,
    value_weight,
    output_weight,
    gate_weight,
    up_matrix,
    down_weight,
):
    s = lax.axis_index("shard")
    y = lax.axis_index("context")
    z = lax.axis_index("tensor")
    order = xor_order(count)
    deep = first_gain.shape[0]
    width = deep * count

    def to_xor(rows):
        return jnp.concatenate(
            [lax.dynamic_slice_in_dim(rows, (s ^ o) * deep, deep, axis=1) for o in order], axis=1
        )

    inverse_order = [order.index(o) for o in range(count)]

    def from_xor(rows):
        slots = jnp.array(inverse_order, jnp.int32)
        return jnp.concatenate(
            [
                lax.dynamic_slice_in_dim(rows, slots[s ^ b] * deep, deep, axis=1)
                for b in range(count)
            ],
            axis=1,
        )

    def swap(halves):
        middle = halves.shape[1] // 2
        return jnp.concatenate([halves[:, middle:], halves[:, :middle]], axis=1)

    def own_first(halves):
        return jnp.where(y == 0, halves, swap(halves))

    meta = jnp.stack([y, z]).astype(jnp.int32)
    positions, starts = positions_of(segments[0])
    start_col = starts[:, None]
    cos, sin = rope_tables(positions)

    bits = shard_bits(count)
    line = Order()

    def fetch(piece, axis=0):
        return [piece, xor_send(piece, bits[0], count)]

    def fetch_end(blocks, axis=0):
        for bit in bits[1:]:
            if count > 4:
                blocks = [jnp.concatenate(blocks, axis=axis)]
            blocks = blocks + [xor_send(b, bit, count) for b in blocks]
        return jnp.concatenate(blocks, axis=axis)

    pack = own_first(
        jnp.concatenate(
            [
                piece[:, part * piece.shape[1] // 2 : (part + 1) * piece.shape[1] // 2]
                for part in range(2)
                for piece in (query_weight, key_weight, value_weight)
            ],
            axis=1,
        )
    )
    out_piece = own_first(output_weight)

    rows = to_xor(tokens[0])
    near = gather_rows_start(rows)
    pack_blocks = fetch(pack)
    gains = jnp.stack([first_gain.astype(F32), second_gain.astype(F32)])
    gains = fetch_end(fetch(gains, 1), 1)
    gain_one, gain_two = gains[:1], gains[1:]
    cot = to_xor(cotangent[0])

    pack_blocks = line.wait(pack_blocks)
    out_blocks = fetch(line.after(out_piece))
    gate_blocks = fetch(line.after(gate_weight))
    w_pack = fetch_end(pack_blocks)
    near = line.wait(near)
    far = gather_rows_next(near)
    out_blocks = line.wait(out_blocks)
    up_blocks = fetch(line.after(up_matrix))
    w_out = fetch_end(out_blocks)
    far = line.wait(far)
    rows_all = gather_rows_end(rows, near, far)

    rows_f = rows.astype(F32)
    scale_one = rms_scale(rows_f)
    all_f = rows_all.astype(F32)
    hat_all = all_f * rms_scale(all_f)
    normed_all = (hat_all * gain_one).astype(BF)
    proj = mm(normed_all, w_pack, ((1,), (0,)), BF)
    proj = line.wait(proj)
    proj_own = proj[:, :PW]
    proj_oth = flip(proj[:, PW:])
    cot_near = gather_rows_start(line.after(cot))
    proj_oth = line.wait(proj_oth)
    att_own, att_oth, rot, lse = attn_forward(
        meta, proj_own.astype(F32), proj_oth.astype(F32), start_col, cos, sin
    )
    att_oth = flip(line.wait(att_oth.astype(BF)))
    cot_near = line.wait(cot_near)
    cot_far = gather_rows_next(cot_near)
    att_oth = line.wait(att_oth)
    context = jnp.concatenate([att_own.astype(BF), att_oth], axis=1)
    attn_terms = line.wait(mm(context, w_out, ((1,), (1,)), BF))
    far = sum_rows_start(attn_terms)
    cot_far = line.wait(cot_far)
    cot_all = gather_rows_end(cot, cot_near, cot_far)
    far = line.wait(far)
    near = sum_rows_next(attn_terms, far)
    gate_blocks = line.wait(gate_blocks)
    down_blocks = fetch(line.after(down_weight))
    w_gate = fetch_end(gate_blocks)
    near = line.wait(near)
    attn = sum_rows_end(attn_terms, near)

    hidden_one = rows_f + attn
    scale_two = rms_scale(hidden_one)
    hat_two = hidden_one * scale_two
    normed_two = line.wait((hat_two * gain_two).astype(BF))
    near = line.wait(gather_rows_start(normed_two))
    far = gather_rows_next(near)
    up_blocks = line.wait(up_blocks)
    w_up = fetch_end(up_blocks)
    far = line.wait(far)
    normed_two_all = gather_rows_end(normed_two, near, far)
    down_blocks = line.wait(down_blocks)
    w_down = fetch_end(down_blocks)
    gate = mm(normed_two_all, w_gate, ((1,), (0,)))
    up = mm(normed_two_all, w_up, ((1,), (0,)))
    sig = jax.nn.sigmoid(gate)
    silu = gate * sig
    hidden = line.wait((silu * up).astype(BF))

    def grad_start(left, right):
        half = width // 2
        term = mm(left[:, half:], right, ((0,), (0,)), BF)
        sent = xor_send(term, bits[-1], count)
        return mm(left[:, :half], right, ((0,), (0,)), BF), sent

    def grad_next(kept, sent):
        kept = line.wait(add_bf(kept, sent))
        half = kept.shape[0] // 2
        if len(bits) < 2:
            return kept, None
        return kept[:half], xor_send(kept[half:], bits[-2], count)

    def grad_end(kept, sent):
        if sent is not None:
            kept = add_bf(kept, sent)
        kept = line.wait(reduce_rest(kept, bits[:-2][::-1], count))
        return kept, flip(kept)

    def both(pair):
        return pair[0].astype(F32) + pair[1].astype(F32)

    down_pair = grad_start(cot_all, hidden)
    down_half = grad_next(*down_pair)
    grad_hidden = mm(line.after(cot_all), w_down, ((1,), (0,)))
    grad_gate = (grad_hidden * up * sig * (1.0 + gate * (1.0 - sig))).astype(BF)
    grad_up = (grad_hidden * silu).astype(BF)
    grad_gate, grad_up = line.wait((grad_gate, grad_up))
    mid_terms = (mm(grad_gate, w_gate, ((1,), (1,))) + mm(grad_up, w_up, ((1,), (1,)))).astype(BF)
    mid_terms = line.wait(mid_terms)
    far = sum_rows_start(mid_terms)
    normed_left, grad_gate = line.after((normed_two_all, grad_gate))
    gate_pair = grad_start(normed_left, grad_gate)
    far = line.wait(far)
    near = sum_rows_next(mid_terms, far)
    down_half = line.wait(down_half)
    down_full = grad_end(*down_half)
    gate_half = grad_next(*gate_pair)
    normed_left, grad_up = line.after((normed_two_all, grad_up))
    up_pair = grad_start(normed_left, grad_up)
    near = line.wait(near)
    normed_two_grad = sum_rows_end(mid_terms, near)

    resid = cot.astype(F32) + norm_backward(normed_two_grad, hat_two, scale_two, gain_two)
    gain_two_part = jnp.sum(normed_two_grad * hat_two, axis=0)

    resid_low = line.wait(resid.astype(BF))
    near = gather_rows_start(resid_low)
    ffn_terms = mm(line.after(hidden), w_down, ((1,), (1,)), BF)
    near, ffn_terms = line.wait((near, ffn_terms))
    far = gather_rows_next(near)
    far = line.wait(far)
    resid_all = gather_rows_end(resid_low, near, far)
    grad_context = line.wait(mm(resid_all, w_out, ((1,), (0,)), BF))
    g_own = grad_context[:, :QW]
    g_oth = flip(grad_context[:, QW:])
    ffn_far = sum_rows_start(line.after(ffn_terms))
    gate_half = line.wait(gate_half)
    gate_full = grad_end(*gate_half)
    up_half = grad_next(*up_pair)
    resid_left, context = line.after((resid_all, context))
    out_pair = grad_start(resid_left, context)
    g_oth = line.wait(g_oth)
    d_own, d_oth = attn_backward(
        meta, rot, lse, g_own.astype(F32), g_oth.astype(F32), start_col, cos, sin
    )
    d_oth = flip(line.wait(d_oth.astype(BF)))
    ffn_far = line.wait(ffn_far)
    ffn_near = sum_rows_next(ffn_terms, ffn_far)
    down_full = line.wait(down_full)
    down_total = both(down_full)
    out_half = grad_next(*out_pair)
    d_oth = line.wait(d_oth)
    d_pack = jnp.concatenate([d_own.astype(BF), d_oth], axis=1)
    one_terms = mm(d_pack, w_pack, ((1,), (1,)))
    ffn_near = line.wait(ffn_near)
    one_low = line.wait(one_terms.astype(BF))
    far = sum_rows_start(one_low)
    up_half = line.wait(up_half)
    up_full = grad_end(*up_half)
    normed_left, d_pack = line.after((normed_all, d_pack))
    pack_pair = grad_start(normed_left, d_pack)
    layer_output = (hidden_one + sum_rows_end(ffn_terms, ffn_near)).astype(BF)
    gain_one_part = jnp.sum(one_terms * hat_all, axis=0)
    far = line.wait(far)
    near = sum_rows_next(one_low, far)
    out_half = line.wait(out_half)
    out_full = grad_end(*out_half)
    pack_half = grad_next(*pack_pair)
    gate_total = both(line.wait(gate_full))

    part = jnp.stack([gain_one_part, gain_two_part])
    for step in (1, 2):
        part = part + lax.ppermute(part, "tensor", [(i, i ^ step) for i in range(4)])
    size = width
    for bit in bits[::-1]:
        size = size // 2
        part = part[:, :size] + xor_send(part[:, size:], bit, count)
    gain_total = part + flip(part)

    pack_half = line.wait(pack_half)
    pack_full = grad_end(*pack_half)
    near = line.wait(near)
    normed_one_grad = sum_rows_end(one_low, near)
    back = norm_backward(normed_one_grad, rows_f * scale_one, scale_one, gain_one)
    tokens_grad = (resid + back).astype(BF)

    def both_swapped(pair):
        return own_first(pair[0].astype(F32) + swap(pair[1]).astype(F32))

    up_total = both(line.wait(up_full))
    out_total = both_swapped(line.wait(out_full))
    pack_total = both_swapped(pack_full)
    query_parts, key_parts, value_parts = (
        jnp.concatenate([pack_total[:, at : at + size], pack_total[:, PW + at : PW + at + size]], 1)
        for at, size in ((0, QW), (QW, HD), (QW + HD, HD))
    )
    return (
        from_xor(layer_output)[None],
        from_xor(tokens_grad)[None],
        gain_total[0],
        gain_total[1],
        query_parts,
        key_parts,
        value_parts,
        out_total,
        gate_total,
        up_total,
        down_total,
    )


def solution(mesh):
    return jax.shard_map(
        functools.partial(shards, mesh.shape["shard"]),
        mesh=mesh,
        in_specs=(
            P("shard", ("context", "tensor"), None),
            P("shard", ("context", "tensor"), None),
            P("shard", None),
            P("shard"),
            P("shard"),
            P("shard", "tensor"),
            P("shard", "tensor"),
            P("shard", "tensor"),
            P("shard", "tensor"),
            P("shard", "tensor"),
            P("shard", "tensor"),
            P("shard", "tensor"),
        ),
        out_specs=(
            P("shard", ("context", "tensor"), None),
            P("shard", ("context", "tensor"), None),
            P("shard"),
            P("shard"),
            P("shard", "tensor"),
            P("shard", "tensor"),
            P("shard", "tensor"),
            P("shard", "tensor"),
            P("shard", "tensor"),
            P("shard", "tensor"),
            P("shard", "tensor"),
        ),
        check_vma=False,
    )
```

```python
import functools

import jax
import jax.numpy as jnp
from jax import lax
from jax.experimental import pallas as pl
from jax.experimental.pallas import tpu as pltpu
from jax.sharding import PartitionSpec as P

H = 32
KV = 8
HD = 64
GROUP = H // KV
QW = GROUP * HD
PW = QW + 2 * HD

EPS = 1e-05
THETA = 500000.0
MASKED = -1e30
BF = jnp.bfloat16
F32 = jnp.float32


def mm(a, b, dims, out=F32):
    return lax.dot_general(a, b, (dims, ((), ())), preferred_element_type=F32).astype(out)


def shift(values, step):
    return lax.ppermute(values, "tensor", [(i, (i + step) % 4) for i in range(4)])


def flip(values):
    return lax.ppermute(values, "context", [(0, 1), (1, 0)])


def xor_send(values, bit, count):
    return lax.ppermute(values, "shard", [(i, i ^ bit) for i in range(count)])


def shard_bits(count):
    bits = []
    bit = count // 2
    while bit:
        bits.append(bit)
        bit //= 2
    return bits


def xor_order(count):
    order = [0]
    for bit in shard_bits(count):
        order = order + [o | bit for o in order]
    return order


class Order:
    def __init__(self):
        self.mark = jnp.zeros((), F32)

    def after(self, values):
        values, self.mark = lax.optimization_barrier((values, self.mark))
        return values

    wait = after


def add_bf(a, b):
    return (a.astype(F32) + b.astype(F32)).astype(BF)


def reduce_rest(kept, bits, count):
    for bit in bits:
        half = kept.shape[0] // 2
        kept = add_bf(kept[:half], xor_send(kept[half:], bit, count))
    return kept


def split_at(rows):
    return -(-rows // 32) * 16


def gather_rows_start(rows):
    return shift(rows, 1), shift(rows, -1)


def gather_rows_next(near):
    right, left = near
    mid = split_at(left.shape[0])
    return shift(left[:mid], -1), shift(right[mid:], 1)


def gather_rows_end(rows, near, far):
    return jnp.concatenate([rows, near[1], far[0], far[1], near[0]], axis=0)


def sum_rows_start(terms):
    length = terms.shape[0] // 4
    mid = split_at(length)
    far = terms[2 * length : 3 * length]
    return shift(far[:mid], 1), shift(far[mid:], -1)


def sum_rows_next(terms, far):
    length = terms.shape[0] // 4
    mid = split_at(length)
    t1, t3 = terms[length : 2 * length], terms[3 * length :]
    t1 = jnp.concatenate([add_bf(t1[:mid], far[0]), t1[mid:]], axis=0)
    t3 = jnp.concatenate([t3[:mid], add_bf(t3[mid:], far[1])], axis=0)
    return shift(t1, 1), shift(t3, -1)


def sum_rows_end(terms, near):
    own = terms[: terms.shape[0] // 4]
    return own.astype(F32) + near[0].astype(F32) + near[1].astype(F32)


def pick_turn(values):
    lane = lax.broadcasted_iota(jnp.int32, values.shape, 1)
    ahead = pltpu.roll(values, 2 * HD - HD // 2, 1)
    behind = pltpu.roll(values, HD // 2, 1)
    return jnp.where(lane % HD < HD // 2, ahead, behind)


def slot_of(block, z, length):
    return pl.multiple_of(((block - z + 4) % 4) * length, 16)


def causal_width(block, length, total):
    return min(total, -(-((block + 1) * length) // 128) * 128)


def masked_scores(q, k, start, first_row):
    s = mm(q, k, ((1,), (1,)))
    col = lax.broadcasted_iota(jnp.int32, s.shape, 1)
    row = lax.broadcasted_iota(jnp.int32, s.shape, 0) + first_row
    return jnp.where((col <= row) & (col >= start), s, MASKED)


def attn_forward_kernel(meta, own, oth, start, cos, sin, att_own, att_oth, rot, lse, nat):
    y, z = meta[0], meta[1]
    total = rot.shape[0]
    half = total // 2
    length = half // 4
    for src, base in ((own, y * half), (oth, (1 - y) * half)):
        for b in range(4):
            at = pl.ds(pl.multiple_of(base + b * length, 16), length)
            rows = src[pl.ds(slot_of(b, z, length), length), :].astype(BF)
            c, s = cos[at, :], sin[at, :]
            for part in range(PW // 128):
                u = rows[:, part * 128 : (part + 1) * 128].astype(F32)
                turned = u * c + pick_turn(u) * s
                if part == PW // 128 - 1:
                    lane = lax.broadcasted_iota(jnp.int32, u.shape, 1)
                    turned = jnp.where(lane < HD, turned, u)
                rot[at, part * 128 : (part + 1) * 128] = turned.astype(BF).astype(F32)
    for b in range(8):
        at = slice(b * length, (b + 1) * length)
        width = causal_width(b, length, total)
        k = rot[:width, QW : QW + HD].astype(BF)
        v = rot[:width, QW + HD :].astype(BF)
        heads = []
        for h in range(GROUP):
            q = (rot[at, h * HD : (h + 1) * HD] * HD**-0.5).astype(BF)
            s = masked_scores(q, k, start[at, :], b * length)
            top = jnp.max(s, axis=1, keepdims=True)
            p = jnp.exp(s - top)
            norm = jnp.sum(p, axis=1, keepdims=True)
            lse[at, h : h + 1] = top + jnp.log(norm)
            p = (p * (1.0 / norm)).astype(BF)
            heads.append(mm(p, v, ((1,), (0,))))
        nat[at, :] = jnp.concatenate(heads, axis=1)
    for dst, base in ((att_own, y * half), (att_oth, (1 - y) * half)):
        for b in range(4):
            at = pl.ds(pl.multiple_of(base + b * length, 16), length)
            dst[pl.ds(slot_of(b, z, length), length), :] = nat[at, :]


def attn_backward_kernel(
    meta, rot, lse, own, oth, start, cos, sin, d_own, d_oth, nat, d_nat, dk, dv
):
    y, z = meta[0], meta[1]
    total = rot.shape[0]
    half = total // 2
    length = half // 4
    for src, base in ((own, y * half), (oth, (1 - y) * half)):
        for b in range(4):
            at = pl.ds(pl.multiple_of(base + b * length, 16), length)
            nat[at, :] = src[pl.ds(slot_of(b, z, length), length), :]
    dk[...] = jnp.zeros_like(dk)
    dv[...] = jnp.zeros_like(dv)
    for b in range(8):
        at = slice(b * length, (b + 1) * length)
        width = causal_width(b, length, total)
        k = rot[:width, QW : QW + HD].astype(BF)
        v = rot[:width, QW + HD :].astype(BF)
        d_heads = []
        for h in range(GROUP):
            q = (rot[at, h * HD : (h + 1) * HD] * HD**-0.5).astype(BF)
            g = nat[at, h * HD : (h + 1) * HD].astype(BF)
            p = jnp.exp(masked_scores(q, k, start[at, :], b * length) - lse[at, h : h + 1])
            dp = mm(g, v, ((1,), (1,)))
            delta = jnp.sum(p * dp, axis=1, keepdims=True)
            ds = (p * (dp - delta)).astype(BF)
            d_heads.append(mm(ds, k, ((1,), (0,))) * HD**-0.5)
            dk[:width, :] += mm(ds, q, ((0,), (0,)))
            dv[:width, :] += mm(p.astype(BF), g, ((0,), (0,)))
        d_q = jnp.concatenate(d_heads, axis=1)
        for part in range(QW // 128):
            u = d_q[:, part * 128 : (part + 1) * 128]
            u = u * cos[at, :] - pick_turn(u) * sin[at, :]
            d_nat[at, part * 128 : (part + 1) * 128] = u
    for b in range(8):
        at = slice(b * length, (b + 1) * length)
        u = jnp.concatenate([dk[at, :], dv[at, :]], axis=1)
        turned = u * cos[at, :] - pick_turn(u) * sin[at, :]
        lane = lax.broadcasted_iota(jnp.int32, u.shape, 1)
        d_nat[at, QW:] = jnp.where(lane < HD, turned, u)
    for dst, base in ((d_own, y * half), (d_oth, (1 - y) * half)):
        for b in range(4):
            at = pl.ds(pl.multiple_of(base + b * length, 16), length)
            dst[pl.ds(slot_of(b, z, length), length), :] = d_nat[at, :]


VMEM = pl.BlockSpec(memory_space=pltpu.VMEM)
SMEM = pl.BlockSpec(memory_space=pltpu.SMEM)
ATTN_PARAMS = dict(vmem_limit_bytes=24 * 1024 * 1024)


def attn_forward(meta, own, oth, start, cos, sin):
    half = own.shape[0]
    return pl.pallas_call(
        attn_forward_kernel,
        out_shape=(
            jax.ShapeDtypeStruct((half, QW), F32),
            jax.ShapeDtypeStruct((half, QW), F32),
            jax.ShapeDtypeStruct((2 * half, PW), F32),
            jax.ShapeDtypeStruct((2 * half, GROUP), F32),
        ),
        in_specs=[SMEM] + [VMEM] * 5,
        out_specs=[VMEM] * 4,
        scratch_shapes=[pltpu.VMEM((2 * half, QW), F32)],
        compiler_params=pltpu.CompilerParams(**ATTN_PARAMS),
        cost_estimate=pl.CostEstimate(
            flops=half * half * QW, bytes_accessed=half * PW, transcendentals=0
        ),
        name="attend_forward",
    )(meta, own, oth, start, cos, sin)


def attn_backward(meta, rot, lse, own, oth, start, cos, sin):
    half = own.shape[0]
    return pl.pallas_call(
        attn_backward_kernel,
        out_shape=(
            jax.ShapeDtypeStruct((half, PW), F32),
            jax.ShapeDtypeStruct((half, PW), F32),
        ),
        in_specs=[SMEM] + [VMEM] * 7,
        out_specs=[VMEM] * 2,
        scratch_shapes=[
            pltpu.VMEM((2 * half, QW), F32),
            pltpu.VMEM((2 * half, PW), F32),
            pltpu.VMEM((2 * half, HD), F32),
            pltpu.VMEM((2 * half, HD), F32),
        ],
        compiler_params=pltpu.CompilerParams(**ATTN_PARAMS),
        cost_estimate=pl.CostEstimate(
            flops=half * half * QW, bytes_accessed=half * PW, transcendentals=0
        ),
        name="attend_backward",
    )(meta, rot, lse, own, oth, start, cos, sin)


def positions_of(seg_row):
    index_row = jnp.arange(seg_row.shape[0], dtype=jnp.int32)
    changed = jnp.concatenate([jnp.ones((1,), bool), seg_row[1:] != seg_row[:-1]])
    starts = lax.cummax(jnp.where(changed, index_row, 0), axis=0)
    return index_row - starts, starts


def rope_tables(positions):
    freq_index = jnp.arange(HD // 2, dtype=F32)
    inverse = THETA ** (-2.0 * freq_index / HD)
    angles = positions.astype(F32)[:, None] * inverse[None, :]
    cosines = jnp.cos(angles)
    sines = jnp.sin(angles)
    return (
        jnp.concatenate([cosines] * 4, axis=-1),
        jnp.concatenate([-sines, sines] * 2, axis=-1),
    )


def rms_scale(values):
    return lax.rsqrt(jnp.mean(values * values, axis=-1, keepdims=True) + EPS)


def norm_backward(grad_normed, normalized, scales, gain):
    rescaled = grad_normed * gain
    grad_input = scales * (
        rescaled - normalized * jnp.mean(rescaled * normalized, axis=-1, keepdims=True)
    )
    return grad_input


def shards(
    count,
    tokens,
    cotangent,
    segments,
    first_gain,
    second_gain,
    query_weight,
    key_weight,
    value_weight,
    output_weight,
    gate_weight,
    up_matrix,
    down_weight,
):
    s = lax.axis_index("shard")
    y = lax.axis_index("context")
    z = lax.axis_index("tensor")
    order = xor_order(count)
    deep = first_gain.shape[0]
    width = deep * count

    def to_xor(rows):
        return jnp.concatenate(
            [lax.dynamic_slice_in_dim(rows, (s ^ o) * deep, deep, axis=1) for o in order], axis=1
        )

    inverse_order = [order.index(o) for o in range(count)]

    def from_xor(rows):
        slots = jnp.array(inverse_order, jnp.int32)
        return jnp.concatenate(
            [
                lax.dynamic_slice_in_dim(rows, slots[s ^ b] * deep, deep, axis=1)
                for b in range(count)
            ],
            axis=1,
        )

    def swap(halves):
        middle = halves.shape[1] // 2
        return jnp.concatenate([halves[:, middle:], halves[:, :middle]], axis=1)

    def own_first(halves):
        return jnp.where(y == 0, halves, swap(halves))

    meta = jnp.stack([y, z]).astype(jnp.int32)
    positions, starts = positions_of(segments[0])
    start_col = starts[:, None]
    cos, sin = rope_tables(positions)

    bits = shard_bits(count)
    line = Order()

    def fetch(piece, axis=0):
        return [piece, xor_send(piece, bits[0], count)]

    def fetch_end(blocks, axis=0):
        for bit in bits[1:]:
            if count > 4:
                blocks = [jnp.concatenate(blocks, axis=axis)]
            blocks = blocks + [xor_send(b, bit, count) for b in blocks]
        return jnp.concatenate(blocks, axis=axis)

    pack = own_first(
        jnp.concatenate(
            [
                piece[:, part * piece.shape[1] // 2 : (part + 1) * piece.shape[1] // 2]
                for part in range(2)
                for piece in (query_weight, key_weight, value_weight)
            ],
            axis=1,
        )
    )
    out_piece = own_first(output_weight)

    rows = to_xor(tokens[0])
    near = gather_rows_start(rows)
    pack_blocks = fetch(pack)
    gains = jnp.stack([first_gain.astype(F32), second_gain.astype(F32)])
    gains = fetch_end(fetch(gains, 1), 1)
    gain_one, gain_two = gains[:1], gains[1:]
    cot = to_xor(cotangent[0])

    pack_blocks = line.wait(pack_blocks)
    out_blocks = fetch(line.after(out_piece))
    w_pack = fetch_end(pack_blocks)
    near = line.wait(near)
    far = gather_rows_next(near)
    out_blocks = line.wait(out_blocks)
    gate_blocks = fetch(line.after(gate_weight))
    w_out = fetch_end(out_blocks)
    far = line.wait(far)
    rows_all = gather_rows_end(rows, near, far)

    rows_f = rows.astype(F32)
    scale_one = rms_scale(rows_f)
    all_f = rows_all.astype(F32)
    hat_all = all_f * rms_scale(all_f)
    normed_all = (hat_all * gain_one).astype(BF)
    proj = line.wait(mm(normed_all, w_pack, ((1,), (0,)), BF))
    proj_own = proj[:, :PW]
    proj_oth = flip(proj[:, PW:])
    cot_near = gather_rows_start(line.after(cot))
    proj_oth = line.wait(proj_oth)
    att_own, att_oth, rot, lse = attn_forward(
        meta, proj_own.astype(F32), proj_oth.astype(F32), start_col, cos, sin
    )
    att_oth = flip(line.wait(att_oth.astype(BF)))
    cot_near = line.wait(cot_near)
    gate_blocks = line.wait(gate_blocks)
    up_blocks = fetch(line.after(up_matrix))
    w_gate = fetch_end(gate_blocks)
    att_oth = line.wait(att_oth)
    context = jnp.concatenate([att_own.astype(BF), att_oth], axis=1)
    attn_terms = line.wait(mm(context, w_out, ((1,), (1,)), BF))
    far = sum_rows_start(attn_terms)
    far = line.wait(far)
    near = sum_rows_next(attn_terms, far)
    up_blocks = line.wait(up_blocks)
    down_blocks = fetch(line.after(down_weight))
    w_up = fetch_end(up_blocks)
    near = line.wait(near)
    attn = sum_rows_end(attn_terms, near)

    hidden_one = rows_f + attn
    scale_two = rms_scale(hidden_one)
    hat_two = hidden_one * scale_two
    normed_two = line.wait((hat_two * gain_two).astype(BF))
    near = line.wait(gather_rows_start(normed_two))
    far = line.wait(gather_rows_next(near))
    cot_far = gather_rows_next(line.after(cot_near))
    normed_two_all = gather_rows_end(normed_two, near, far)
    gate = mm(normed_two_all, w_gate, ((1,), (0,)))
    down_blocks, gate = line.wait((down_blocks, gate))
    w_down = fetch_end(down_blocks)
    up = mm(normed_two_all, w_up, ((1,), (0,)))
    sig = jax.nn.sigmoid(gate)
    silu = gate * sig
    hidden, cot_far = line.wait(((silu * up).astype(BF), cot_far))
    cot_all = gather_rows_end(cot, cot_near, cot_far)

    def grad_start(left, right):
        half = width // 2
        term = mm(left[:, half:], right, ((0,), (0,)), BF)
        sent = xor_send(term, bits[-1], count)
        return mm(left[:, :half], right, ((0,), (0,)), BF), sent

    def grad_next(kept, sent, pieces):
        kept = line.wait(add_bf(kept, sent))
        if len(bits) != 2:
            return [(reduce_rest(kept, bits[:-1][::-1], count), None)]
        size = kept.shape[0] // 2 // pieces
        return [
            (
                kept[i * size : (i + 1) * size],
                xor_send(kept[(pieces + i) * size : (pieces + i + 1) * size], bits[-2], count),
            )
            for i in range(pieces)
        ]

    def grad_end(halves, at):
        kept, sent = halves[min(at, len(halves) - 1)]
        if sent is not None:
            kept = line.wait(add_bf(kept, line.wait(sent)))
        elif at:
            return None
        return kept, flip(kept)

    def both(pairs):
        return jnp.concatenate([p[0].astype(F32) + p[1].astype(F32) for p in pairs if p], axis=0)

    down_pair = grad_start(cot_all, hidden)
    ffn_terms = mm(hidden, w_down, ((1,), (1,)), BF)
    down_half = grad_next(*down_pair, 2)
    ffn_terms = line.wait(ffn_terms)
    ffn_far = sum_rows_start(ffn_terms)
    grad_hidden = mm(line.after(cot_all), w_down, ((1,), (0,)))
    grad_gate = (grad_hidden * up * sig * (1.0 + gate * (1.0 - sig))).astype(BF)
    grad_up = (grad_hidden * silu).astype(BF)
    grad_gate, grad_up = line.wait((grad_gate, grad_up))
    ffn_far = line.wait(ffn_far)
    ffn_near = sum_rows_next(ffn_terms, ffn_far)
    mid_terms = line.wait(mm(grad_gate, w_gate, ((1,), (1,))))
    down_a = grad_end(down_half, 0)
    mid_terms = line.wait((mid_terms + mm(grad_up, w_up, ((1,), (1,)))).astype(BF))
    far = sum_rows_start(mid_terms)
    normed_left, grad_gate = line.after((normed_two_all, grad_gate))
    gate_pair = grad_start(normed_left, grad_gate)
    down_b = grad_end(down_half, 1)
    gate_half = grad_next(*gate_pair, 2)
    far = line.wait(far)
    near = sum_rows_next(mid_terms, far)
    normed_left, grad_up = line.after((normed_two_all, grad_up))
    up_pair = grad_start(normed_left, grad_up)
    ffn_near = line.wait(ffn_near)
    layer_output = (hidden_one + sum_rows_end(ffn_terms, ffn_near)).astype(BF)
    down_a = line.wait(down_a)
    gate_a = grad_end(gate_half, 0)
    near = line.wait(near)
    normed_two_grad = sum_rows_end(mid_terms, near)

    resid = cot.astype(F32) + norm_backward(normed_two_grad, hat_two, scale_two, gain_two)
    gain_two_part = jnp.sum(normed_two_grad * hat_two, axis=0)

    resid_low = line.wait(resid.astype(BF))
    near = gather_rows_start(resid_low)
    up_half = grad_next(*up_pair, 2)
    gate_b = grad_end(gate_half, 1)
    down_b = line.wait(down_b)
    near = line.wait(near)
    far = gather_rows_next(near)
    gate_a = line.wait(gate_a)
    far = line.wait(far)
    resid_all = gather_rows_end(resid_low, near, far)
    gate_b, grad_context = line.wait((gate_b, mm(resid_all, w_out, ((1,), (0,)), BF)))
    g_own = grad_context[:, :QW]
    g_oth = flip(grad_context[:, QW:])
    resid_left, context = line.after((resid_all, context))
    out_pair = grad_start(resid_left, context)
    g_oth = line.wait(g_oth)
    up_a = grad_end(up_half, 0)
    d_own, d_oth = attn_backward(
        meta, rot, lse, g_own.astype(F32), g_oth.astype(F32), start_col, cos, sin
    )
    up_a, d_oth = line.wait((up_a, d_oth.astype(BF)))
    d_oth = flip(d_oth)
    out_half = grad_next(*out_pair, 1)
    d_oth = line.wait(d_oth)
    up_b = grad_end(up_half, 1)
    d_pack = jnp.concatenate([d_own.astype(BF), d_oth], axis=1)
    one_terms = mm(d_pack, w_pack, ((1,), (1,)))
    one_low = line.wait(one_terms.astype(BF))
    far = sum_rows_start(one_low)
    normed_left, d_pack = line.after((normed_all, d_pack))
    pack_pair = grad_start(normed_left, d_pack)
    out_full = grad_end(out_half, 0)
    pack_half = grad_next(*pack_pair, 1)
    far = line.wait(far)
    near = sum_rows_next(one_low, far)
    gain_one_part = jnp.sum(one_terms * hat_all, axis=0)
    part = line.wait(jnp.stack([gain_one_part, gain_two_part]))

    part = line.wait(part + lax.ppermute(part, "tensor", [(i, i ^ 1) for i in range(4)]))
    down_total = both(line.wait([down_a, down_b]))
    part = line.wait(part + lax.ppermute(part, "tensor", [(i, i ^ 2) for i in range(4)]))
    pack_full = grad_end(pack_half, 0)
    size = width
    for bit in bits[::-1]:
        size = size // 2
        part = line.wait(part[:, :size] + xor_send(part[:, size:], bit, count))
    gain_total = part + flip(part)
    gate_total = both(line.wait([gate_a, gate_b]))

    near = line.wait(near)
    normed_one_grad = sum_rows_end(one_low, near)
    back = norm_backward(normed_one_grad, rows_f * scale_one, scale_one, gain_one)
    tokens_grad = (resid + back).astype(BF)

    def both_swapped(pair):
        return own_first(pair[0].astype(F32) + swap(pair[1]).astype(F32))

    up_total = both(line.wait([up_a, up_b]))
    out_total = both_swapped(line.wait(out_full))
    pack_total = both_swapped(pack_full)
    query_parts, key_parts, value_parts = (
        jnp.concatenate([pack_total[:, at : at + size], pack_total[:, PW + at : PW + at + size]], 1)
        for at, size in ((0, QW), (QW, HD), (QW + HD, HD))
    )
    return (
        from_xor(layer_output)[None],
        from_xor(tokens_grad)[None],
        gain_total[0] + line.mark,
        gain_total[1],
        query_parts,
        key_parts,
        value_parts,
        out_total,
        gate_total,
        up_total,
        down_total,
    )


def solution(mesh):
    return jax.shard_map(
        functools.partial(shards, mesh.shape["shard"]),
        mesh=mesh,
        in_specs=(
            P("shard", ("context", "tensor"), None),
            P("shard", ("context", "tensor"), None),
            P("shard", None),
            P("shard"),
            P("shard"),
            P("shard", "tensor"),
            P("shard", "tensor"),
            P("shard", "tensor"),
            P("shard", "tensor"),
            P("shard", "tensor"),
            P("shard", "tensor"),
            P("shard", "tensor"),
        ),
        out_specs=(
            P("shard", ("context", "tensor"), None),
            P("shard", ("context", "tensor"), None),
            P("shard"),
            P("shard"),
            P("shard", "tensor"),
            P("shard", "tensor"),
            P("shard", "tensor"),
            P("shard", "tensor"),
            P("shard", "tensor"),
            P("shard", "tensor"),
            P("shard", "tensor"),
        ),
        check_vma=False,
    )
```

```python
import functools

import jax
import jax.numpy as jnp
from jax import lax
from jax.experimental import pallas as pl
from jax.experimental.pallas import tpu as pltpu
from jax.sharding import PartitionSpec as P

H = 32
KV = 8
HD = 64
GROUP = H // KV
QW = GROUP * HD
PW = QW + 2 * HD

EPS = 1e-05
THETA = 500000.0
MASKED = -1e30
BF = jnp.bfloat16
F32 = jnp.float32


def mm(a, b, dims, out=F32):
    return lax.dot_general(a, b, (dims, ((), ())), preferred_element_type=F32).astype(out)


def shift(values, step):
    return lax.ppermute(values, "tensor", [(i, (i + step) % 4) for i in range(4)])


def flip(values):
    return lax.ppermute(values, "context", [(0, 1), (1, 0)])


def xor_send(values, bit, count):
    return lax.ppermute(values, "shard", [(i, i ^ bit) for i in range(count)])


def shard_bits(count):
    bits = []
    bit = count // 2
    while bit:
        bits.append(bit)
        bit //= 2
    return bits


def xor_order(count):
    order = [0]
    for bit in shard_bits(count):
        order = order + [o | bit for o in order]
    return order


class Order:
    def __init__(self):
        self.mark = jnp.zeros((), F32)

    def after(self, values):
        values, self.mark = lax.optimization_barrier((values, self.mark))
        return values

    wait = after


def add_bf(a, b):
    return (a.astype(F32) + b.astype(F32)).astype(BF)


def reduce_rest(kept, bits, count):
    for bit in bits:
        half = kept.shape[0] // 2
        kept = add_bf(kept[:half], xor_send(kept[half:], bit, count))
    return kept


def split_at(rows):
    return -(-rows // 32) * 16


def gather_rows_start(rows):
    return shift(rows, 1), shift(rows, -1)


def gather_rows_next(near):
    right, left = near
    mid = split_at(left.shape[0])
    return shift(left[:mid], -1), shift(right[mid:], 1)


def gather_rows_end(rows, near, far):
    return jnp.concatenate([rows, near[1], far[0], far[1], near[0]], axis=0)


def sum_rows_start(terms):
    length = terms.shape[0] // 4
    mid = split_at(length)
    far = terms[2 * length : 3 * length]
    return shift(far[:mid], 1), shift(far[mid:], -1)


def sum_rows_next(terms, far):
    length = terms.shape[0] // 4
    mid = split_at(length)
    t1, t3 = terms[length : 2 * length], terms[3 * length :]
    t1 = jnp.concatenate([add_bf(t1[:mid], far[0]), t1[mid:]], axis=0)
    t3 = jnp.concatenate([t3[:mid], add_bf(t3[mid:], far[1])], axis=0)
    return shift(t1, 1), shift(t3, -1)


def sum_rows_end(terms, near):
    own = terms[: terms.shape[0] // 4]
    return own.astype(F32) + near[0].astype(F32) + near[1].astype(F32)


def pick_turn(values):
    lane = lax.broadcasted_iota(jnp.int32, values.shape, 1)
    ahead = pltpu.roll(values, 2 * HD - HD // 2, 1)
    behind = pltpu.roll(values, HD // 2, 1)
    return jnp.where(lane % HD < HD // 2, ahead, behind)


def slot_of(block, z, length):
    return pl.multiple_of(((block - z + 4) % 4) * length, 16)


def causal_width(block, length, total):
    return min(total, -(-((block + 1) * length) // 128) * 128)


def masked_scores(q, k, start, first_row):
    s = mm(q, k, ((1,), (1,)))
    col = lax.broadcasted_iota(jnp.int32, s.shape, 1)
    row = lax.broadcasted_iota(jnp.int32, s.shape, 0) + first_row
    return jnp.where((col <= row) & (col >= start), s, MASKED)


def attn_forward_kernel(meta, own, oth, start, cos, sin, att_own, att_oth, rot, lse, nat):
    y, z = meta[0], meta[1]
    total = rot.shape[0]
    half = total // 2
    length = half // 4
    for src, base in ((own, y * half), (oth, (1 - y) * half)):
        for b in range(4):
            at = pl.ds(pl.multiple_of(base + b * length, 16), length)
            rows = src[pl.ds(slot_of(b, z, length), length), :].astype(BF)
            c, s = cos[at, :], sin[at, :]
            for part in range(PW // 128):
                u = rows[:, part * 128 : (part + 1) * 128].astype(F32)
                turned = u * c + pick_turn(u) * s
                if part == PW // 128 - 1:
                    lane = lax.broadcasted_iota(jnp.int32, u.shape, 1)
                    turned = jnp.where(lane < HD, turned, u)
                rot[at, part * 128 : (part + 1) * 128] = turned.astype(BF).astype(F32)
    for b in range(8):
        at = slice(b * length, (b + 1) * length)
        width = causal_width(b, length, total)
        k = rot[:width, QW : QW + HD].astype(BF)
        v = rot[:width, QW + HD :].astype(BF)
        heads = []
        for h in range(GROUP):
            q = (rot[at, h * HD : (h + 1) * HD] * HD**-0.5).astype(BF)
            s = masked_scores(q, k, start[at, :], b * length)
            top = jnp.max(s, axis=1, keepdims=True)
            p = jnp.exp(s - top)
            norm = jnp.sum(p, axis=1, keepdims=True)
            lse[at, h : h + 1] = top + jnp.log(norm)
            p = (p * (1.0 / norm)).astype(BF)
            heads.append(mm(p, v, ((1,), (0,))))
        nat[at, :] = jnp.concatenate(heads, axis=1)
    for dst, base in ((att_own, y * half), (att_oth, (1 - y) * half)):
        for b in range(4):
            at = pl.ds(pl.multiple_of(base + b * length, 16), length)
            dst[pl.ds(slot_of(b, z, length), length), :] = nat[at, :]


def attn_backward_kernel(
    meta, rot, lse, own, oth, start, cos, sin, d_own, d_oth, nat, d_nat, dk, dv
):
    y, z = meta[0], meta[1]
    total = rot.shape[0]
    half = total // 2
    length = half // 4
    for src, base in ((own, y * half), (oth, (1 - y) * half)):
        for b in range(4):
            at = pl.ds(pl.multiple_of(base + b * length, 16), length)
            nat[at, :] = src[pl.ds(slot_of(b, z, length), length), :]
    dk[...] = jnp.zeros_like(dk)
    dv[...] = jnp.zeros_like(dv)
    for b in range(8):
        at = slice(b * length, (b + 1) * length)
        width = causal_width(b, length, total)
        k = rot[:width, QW : QW + HD].astype(BF)
        v = rot[:width, QW + HD :].astype(BF)
        d_heads = []
        for h in range(GROUP):
            q = (rot[at, h * HD : (h + 1) * HD] * HD**-0.5).astype(BF)
            g = nat[at, h * HD : (h + 1) * HD].astype(BF)
            p = jnp.exp(masked_scores(q, k, start[at, :], b * length) - lse[at, h : h + 1])
            dp = mm(g, v, ((1,), (1,)))
            delta = jnp.sum(p * dp, axis=1, keepdims=True)
            ds = (p * (dp - delta)).astype(BF)
            d_heads.append(mm(ds, k, ((1,), (0,))) * HD**-0.5)
            dk[:width, :] += mm(ds, q, ((0,), (0,)))
            dv[:width, :] += mm(p.astype(BF), g, ((0,), (0,)))
        d_q = jnp.concatenate(d_heads, axis=1)
        for part in range(QW // 128):
            u = d_q[:, part * 128 : (part + 1) * 128]
            u = u * cos[at, :] - pick_turn(u) * sin[at, :]
            d_nat[at, part * 128 : (part + 1) * 128] = u
    for b in range(8):
        at = slice(b * length, (b + 1) * length)
        u = jnp.concatenate([dk[at, :], dv[at, :]], axis=1)
        turned = u * cos[at, :] - pick_turn(u) * sin[at, :]
        lane = lax.broadcasted_iota(jnp.int32, u.shape, 1)
        d_nat[at, QW:] = jnp.where(lane < HD, turned, u)
    for dst, base in ((d_own, y * half), (d_oth, (1 - y) * half)):
        for b in range(4):
            at = pl.ds(pl.multiple_of(base + b * length, 16), length)
            dst[pl.ds(slot_of(b, z, length), length), :] = d_nat[at, :]


VMEM = pl.BlockSpec(memory_space=pltpu.VMEM)
SMEM = pl.BlockSpec(memory_space=pltpu.SMEM)
ATTN_PARAMS = dict(vmem_limit_bytes=24 * 1024 * 1024)


def attn_forward(meta, own, oth, start, cos, sin):
    half = own.shape[0]
    return pl.pallas_call(
        attn_forward_kernel,
        out_shape=(
            jax.ShapeDtypeStruct((half, QW), F32),
            jax.ShapeDtypeStruct((half, QW), F32),
            jax.ShapeDtypeStruct((2 * half, PW), F32),
            jax.ShapeDtypeStruct((2 * half, GROUP), F32),
        ),
        in_specs=[SMEM] + [VMEM] * 5,
        out_specs=[VMEM] * 4,
        scratch_shapes=[pltpu.VMEM((2 * half, QW), F32)],
        compiler_params=pltpu.CompilerParams(**ATTN_PARAMS),
        cost_estimate=pl.CostEstimate(
            flops=half * half * QW, bytes_accessed=half * PW, transcendentals=0
        ),
        name="attend_forward",
    )(meta, own, oth, start, cos, sin)


def attn_backward(meta, rot, lse, own, oth, start, cos, sin):
    half = own.shape[0]
    return pl.pallas_call(
        attn_backward_kernel,
        out_shape=(
            jax.ShapeDtypeStruct((half, PW), F32),
            jax.ShapeDtypeStruct((half, PW), F32),
        ),
        in_specs=[SMEM] + [VMEM] * 7,
        out_specs=[VMEM] * 2,
        scratch_shapes=[
            pltpu.VMEM((2 * half, QW), F32),
            pltpu.VMEM((2 * half, PW), F32),
            pltpu.VMEM((2 * half, HD), F32),
            pltpu.VMEM((2 * half, HD), F32),
        ],
        compiler_params=pltpu.CompilerParams(**ATTN_PARAMS),
        cost_estimate=pl.CostEstimate(
            flops=half * half * QW, bytes_accessed=half * PW, transcendentals=0
        ),
        name="attend_backward",
    )(meta, rot, lse, own, oth, start, cos, sin)


def positions_of(seg_row):
    index_row = jnp.arange(seg_row.shape[0], dtype=jnp.int32)
    changed = jnp.concatenate([jnp.ones((1,), bool), seg_row[1:] != seg_row[:-1]])
    starts = lax.cummax(jnp.where(changed, index_row, 0), axis=0)
    return index_row - starts, starts


def rope_tables(positions):
    freq_index = jnp.arange(HD // 2, dtype=F32)
    inverse = THETA ** (-2.0 * freq_index / HD)
    angles = positions.astype(F32)[:, None] * inverse[None, :]
    cosines = jnp.cos(angles)
    sines = jnp.sin(angles)
    return (
        jnp.concatenate([cosines] * 4, axis=-1),
        jnp.concatenate([-sines, sines] * 2, axis=-1),
    )


def rms_scale(values):
    return lax.rsqrt(jnp.mean(values * values, axis=-1, keepdims=True) + EPS)


def norm_backward(grad_normed, normalized, scales, gain):
    rescaled = grad_normed * gain
    grad_input = scales * (
        rescaled - normalized * jnp.mean(rescaled * normalized, axis=-1, keepdims=True)
    )
    return grad_input


def shards(
    count,
    tokens,
    cotangent,
    segments,
    first_gain,
    second_gain,
    query_weight,
    key_weight,
    value_weight,
    output_weight,
    gate_weight,
    up_matrix,
    down_weight,
):
    s = lax.axis_index("shard")
    y = lax.axis_index("context")
    z = lax.axis_index("tensor")
    order = xor_order(count)
    deep = first_gain.shape[0]
    width = deep * count

    def to_xor(rows):
        return jnp.concatenate(
            [lax.dynamic_slice_in_dim(rows, (s ^ o) * deep, deep, axis=1) for o in order], axis=1
        )

    inverse_order = [order.index(o) for o in range(count)]

    def from_xor(rows):
        slots = jnp.array(inverse_order, jnp.int32)
        return jnp.concatenate(
            [
                lax.dynamic_slice_in_dim(rows, slots[s ^ b] * deep, deep, axis=1)
                for b in range(count)
            ],
            axis=1,
        )

    def swap(halves):
        middle = halves.shape[1] // 2
        return jnp.concatenate([halves[:, middle:], halves[:, :middle]], axis=1)

    def own_first(halves):
        return jnp.where(y == 0, halves, swap(halves))

    meta = jnp.stack([y, z]).astype(jnp.int32)
    positions, starts = positions_of(segments[0])
    start_col = starts[:, None]
    cos, sin = rope_tables(positions)

    bits = shard_bits(count)
    line = Order()

    def fetch(piece, axis=0):
        return [piece, xor_send(piece, bits[0], count)]

    def fetch_end(blocks, axis=0):
        for bit in bits[1:]:
            if count > 4:
                blocks = [jnp.concatenate(blocks, axis=axis)]
            blocks = blocks + [xor_send(b, bit, count) for b in blocks]
        return jnp.concatenate(blocks, axis=axis)

    pack = own_first(
        jnp.concatenate(
            [
                piece[:, part * piece.shape[1] // 2 : (part + 1) * piece.shape[1] // 2]
                for part in range(2)
                for piece in (query_weight, key_weight, value_weight)
            ],
            axis=1,
        )
    )
    out_piece = own_first(output_weight)

    rows = to_xor(tokens[0])
    near = gather_rows_start(rows)
    pack_blocks = fetch(pack)
    gains = jnp.stack([first_gain.astype(F32), second_gain.astype(F32)])
    gains = fetch_end(fetch(gains, 1), 1)
    gain_one, gain_two = gains[:1], gains[1:]
    cot = to_xor(cotangent[0])

    pack_blocks = line.wait(pack_blocks)
    out_blocks = fetch(line.after(out_piece))
    w_pack = fetch_end(pack_blocks)
    near = line.wait(near)
    far = gather_rows_next(near)
    out_blocks = line.wait(out_blocks)
    gate_blocks = fetch(line.after(gate_weight))
    w_out = fetch_end(out_blocks)
    far = line.wait(far)
    rows_all = gather_rows_end(rows, near, far)

    rows_f = rows.astype(F32)
    scale_one = rms_scale(rows_f)
    all_f = rows_all.astype(F32)
    hat_all = all_f * rms_scale(all_f)
    normed_all = (hat_all * gain_one).astype(BF)
    proj = line.wait(mm(normed_all, w_pack, ((1,), (0,)), BF))
    proj_own = proj[:, :PW]
    proj_oth = flip(proj[:, PW:])
    cot_near = gather_rows_start(line.after(cot))
    proj_oth = line.wait(proj_oth)
    att_own, att_oth, rot, lse = attn_forward(
        meta, proj_own.astype(F32), proj_oth.astype(F32), start_col, cos, sin
    )
    att_oth = flip(line.wait(att_oth.astype(BF)))
    cot_near = line.wait(cot_near)
    gate_blocks = line.wait(gate_blocks)
    up_blocks = fetch(line.after(up_matrix))
    w_gate = fetch_end(gate_blocks)
    att_oth = line.wait(att_oth)
    context = jnp.concatenate([att_own.astype(BF), att_oth], axis=1)
    attn_terms = line.wait(mm(context, w_out, ((1,), (1,)), BF))
    far = sum_rows_start(attn_terms)
    far = line.wait(far)
    near = sum_rows_next(attn_terms, far)
    up_blocks = line.wait(up_blocks)
    down_blocks = fetch(line.after(down_weight))
    w_up = fetch_end(up_blocks)
    near = line.wait(near)
    attn = sum_rows_end(attn_terms, near)

    hidden_one = rows_f + attn
    scale_two = rms_scale(hidden_one)
    hat_two = hidden_one * scale_two
    normed_two = line.wait((hat_two * gain_two).astype(BF))
    near = line.wait(gather_rows_start(normed_two))
    far = line.wait(gather_rows_next(near))
    cot_far = gather_rows_next(line.after(cot_near))
    normed_two_all = gather_rows_end(normed_two, near, far)
    gate = mm(normed_two_all, w_gate, ((1,), (0,)))
    down_blocks, gate = line.wait((down_blocks, gate))
    w_down = fetch_end(down_blocks)
    up = mm(normed_two_all, w_up, ((1,), (0,)))
    sig = jax.nn.sigmoid(gate)
    silu = gate * sig
    hidden, cot_far = line.wait(((silu * up).astype(BF), cot_far))
    cot_all = gather_rows_end(cot, cot_near, cot_far)

    def grad_start(left, right):
        half = width // 2
        term = mm(left[:, half:], right, ((0,), (0,)), BF)
        sent = xor_send(term, bits[-1], count)
        return mm(left[:, :half], right, ((0,), (0,)), BF), sent

    def grad_next(kept, sent, pieces):
        kept = line.wait(add_bf(kept, sent))
        if len(bits) != 2:
            return [(reduce_rest(kept, bits[:-1][::-1], count), None)]
        size = kept.shape[0] // 2 // pieces
        return [
            (
                kept[i * size : (i + 1) * size],
                xor_send(kept[(pieces + i) * size : (pieces + i + 1) * size], bits[-2], count),
            )
            for i in range(pieces)
        ]

    def grad_end(halves, at):
        kept, sent = halves[min(at, len(halves) - 1)]
        if sent is not None:
            kept = line.wait(add_bf(kept, line.wait(sent)))
        elif at:
            return None
        return kept, flip(kept)

    def both(pairs):
        return jnp.concatenate([p[0].astype(F32) + p[1].astype(F32) for p in pairs if p], axis=0)

    down_pair = grad_start(cot_all, hidden)
    down_half = grad_next(*down_pair, 2)
    grad_hidden = mm(line.after(cot_all), w_down, ((1,), (0,)))
    grad_gate = (grad_hidden * up * sig * (1.0 + gate * (1.0 - sig))).astype(BF)
    grad_up = (grad_hidden * silu).astype(BF)
    grad_gate, grad_up = line.wait((grad_gate, grad_up))
    mid_terms = mm(grad_gate, w_gate, ((1,), (1,))) + mm(grad_up, w_up, ((1,), (1,)))
    mid_terms = line.wait(mid_terms.astype(BF))
    far = sum_rows_start(mid_terms)
    far = line.wait(far)
    near = sum_rows_next(mid_terms, far)
    normed_left, grad_gate = line.after((normed_two_all, grad_gate))
    gate_pair = grad_start(normed_left, grad_gate)
    down_a = grad_end(down_half, 0)
    gate_half = grad_next(*gate_pair, 2)
    near = line.wait(near)
    normed_two_grad = sum_rows_end(mid_terms, near)

    resid = cot.astype(F32) + norm_backward(normed_two_grad, hat_two, scale_two, gain_two)
    gain_two_part = jnp.sum(normed_two_grad * hat_two, axis=0)

    resid_low = line.wait(resid.astype(BF))
    near = gather_rows_start(resid_low)
    normed_left, grad_up = line.after((normed_two_all, grad_up))
    up_pair = grad_start(normed_left, grad_up)
    down_b = grad_end(down_half, 1)
    near = line.wait(near)
    far = gather_rows_next(near)
    gate_a = grad_end(gate_half, 0)
    far = line.wait(far)
    resid_all = gather_rows_end(resid_low, near, far)
    grad_context = line.wait(mm(resid_all, w_out, ((1,), (0,)), BF))
    g_own = grad_context[:, :QW]
    g_oth = flip(grad_context[:, QW:])
    ffn_terms = line.wait(mm(line.after(hidden), w_down, ((1,), (1,)), BF))
    ffn_far = sum_rows_start(ffn_terms)
    up_half = grad_next(*up_pair, 2)
    g_oth = line.wait(g_oth)
    gate_b = grad_end(gate_half, 1)
    ffn_far = line.wait(ffn_far)
    ffn_near = sum_rows_next(ffn_terms, ffn_far)
    d_own, d_oth = attn_backward(
        meta, rot, lse, g_own.astype(F32), g_oth.astype(F32), start_col, cos, sin
    )
    down_a, down_b, gate_a, gate_b, ffn_near, d_oth = line.wait(
        (down_a, down_b, gate_a, gate_b, ffn_near, d_oth.astype(BF))
    )
    d_oth = flip(d_oth)
    resid_left, context = line.after((resid_all, context))
    out_pair = grad_start(resid_left, context)
    up_half[0] = line.wait(up_half[0])
    out_half = grad_next(*out_pair, 1)
    layer_output = (hidden_one + sum_rows_end(ffn_terms, ffn_near)).astype(BF)
    layer_output = line.wait(layer_output)
    d_oth = line.wait(d_oth)
    up_a = grad_end(up_half, 0)
    d_pack = jnp.concatenate([d_own.astype(BF), d_oth], axis=1)
    one_terms = mm(d_pack, w_pack, ((1,), (1,)))
    gain_one_part = jnp.sum(one_terms * hat_all, axis=0)
    one_low, part = line.wait((one_terms.astype(BF), jnp.stack([gain_one_part, gain_two_part])))
    far = sum_rows_start(one_low)
    part_terms = [part] + [shift(part, -step) for step in (1, 2, 3)]
    normed_left, d_pack = line.after((normed_all, d_pack))
    pack_pair = grad_start(normed_left, d_pack)
    far = line.wait(far)
    near = sum_rows_next(one_low, far)
    up_b = grad_end(up_half, 1)
    out_full = grad_end(out_half, 0)
    pack_half = grad_next(*pack_pair, 1)

    down_total = both([down_a, down_b])
    pack_full = grad_end(pack_half, 0)
    gate_total = both([gate_a, gate_b])

    near = line.wait(near)
    normed_one_grad = sum_rows_end(one_low, near)
    back = norm_backward(normed_one_grad, rows_f * scale_one, scale_one, gain_one)
    tokens_grad = (resid + back).astype(BF)

    def both_swapped(pair):
        return own_first(pair[0].astype(F32) + swap(pair[1]).astype(F32))

    up_total = both(line.wait([up_a, up_b]))

    part_terms = jnp.stack(part_terms + part_terms)
    part = jnp.sum(lax.dynamic_slice_in_dim(part_terms, (4 - z) % 4, 4, axis=0), axis=0)
    size = width
    for bit in bits[::-1]:
        size = size // 2
        part = part[:, :size] + xor_send(part[:, size:], bit, count)
    gain_total = part + flip(part)
    out_total = both_swapped(line.wait(out_full))
    pack_total = both_swapped(pack_full)
    query_parts, key_parts, value_parts = (
        jnp.concatenate([pack_total[:, at : at + size], pack_total[:, PW + at : PW + at + size]], 1)
        for at, size in ((0, QW), (QW, HD), (QW + HD, HD))
    )
    return (
        from_xor(layer_output)[None],
        from_xor(tokens_grad)[None],
        gain_total[0] + line.mark,
        gain_total[1],
        query_parts,
        key_parts,
        value_parts,
        out_total,
        gate_total,
        up_total,
        down_total,
    )


def solution(mesh):
    return jax.shard_map(
        functools.partial(shards, mesh.shape["shard"]),
        mesh=mesh,
        in_specs=(
            P("shard", ("context", "tensor"), None),
            P("shard", ("context", "tensor"), None),
            P("shard", None),
            P("shard"),
            P("shard"),
            P("shard", "tensor"),
            P("shard", "tensor"),
            P("shard", "tensor"),
            P("shard", "tensor"),
            P("shard", "tensor"),
            P("shard", "tensor"),
            P("shard", "tensor"),
        ),
        out_specs=(
            P("shard", ("context", "tensor"), None),
            P("shard", ("context", "tensor"), None),
            P("shard"),
            P("shard"),
            P("shard", "tensor"),
            P("shard", "tensor"),
            P("shard", "tensor"),
            P("shard", "tensor"),
            P("shard", "tensor"),
            P("shard", "tensor"),
            P("shard", "tensor"),
        ),
        check_vma=False,
    )
```

```python
import functools

import jax
import jax.numpy as jnp
from jax import lax
from jax.experimental import pallas as pl
from jax.experimental.pallas import tpu as pltpu
from jax.sharding import PartitionSpec as P

H = 32
KV = 8
HD = 64
GROUP = H // KV
QW = GROUP * HD
PW = QW + 2 * HD

EPS = 1e-05
THETA = 500000.0
MASKED = -1e30
BF = jnp.bfloat16
F32 = jnp.float32


def mm(a, b, dims, out=F32):
    return lax.dot_general(a, b, (dims, ((), ())), preferred_element_type=F32).astype(out)


def shift(values, step):
    return lax.ppermute(values, "tensor", [(i, (i + step) % 4) for i in range(4)])


def flip(values):
    return lax.ppermute(values, "context", [(0, 1), (1, 0)])


def xor_send(values, bit, count):
    return lax.ppermute(values, "shard", [(i, i ^ bit) for i in range(count)])


def shard_bits(count):
    bits = []
    bit = count // 2
    while bit:
        bits.append(bit)
        bit //= 2
    return bits


def xor_order(count):
    order = [0]
    for bit in shard_bits(count):
        order = order + [o | bit for o in order]
    return order


class Order:
    def __init__(self):
        self.mark = jnp.zeros((), F32)

    def after(self, values):
        values, self.mark = lax.optimization_barrier((values, self.mark))
        return values

    wait = after


def add_bf(a, b):
    return (a.astype(F32) + b.astype(F32)).astype(BF)


def reduce_rest(kept, bits, count):
    for bit in bits:
        half = kept.shape[0] // 2
        kept = add_bf(kept[:half], xor_send(kept[half:], bit, count))
    return kept


def split_at(rows):
    return -(-rows // 32) * 16


def gather_rows_start(rows):
    return shift(rows, 1), shift(rows, -1)


def gather_rows_next(near):
    right, left = near
    mid = split_at(left.shape[0])
    return shift(left[:mid], -1), shift(right[mid:], 1)


def gather_rows_end(rows, near, far):
    return jnp.concatenate([rows, near[1], far[0], far[1], near[0]], axis=0)


def sum_rows_start(terms):
    length = terms.shape[0] // 4
    mid = split_at(length)
    far = terms[2 * length : 3 * length]
    return shift(far[:mid], 1), shift(far[mid:], -1)


def sum_rows_next(terms, far):
    length = terms.shape[0] // 4
    mid = split_at(length)
    t1, t3 = terms[length : 2 * length], terms[3 * length :]
    t1 = jnp.concatenate([add_bf(t1[:mid], far[0]), t1[mid:]], axis=0)
    t3 = jnp.concatenate([t3[:mid], add_bf(t3[mid:], far[1])], axis=0)
    return shift(t1, 1), shift(t3, -1)


def sum_rows_end(terms, near):
    own = terms[: terms.shape[0] // 4]
    return own.astype(F32) + near[0].astype(F32) + near[1].astype(F32)


def pick_turn(values):
    lane = lax.broadcasted_iota(jnp.int32, values.shape, 1)
    ahead = pltpu.roll(values, 2 * HD - HD // 2, 1)
    behind = pltpu.roll(values, HD // 2, 1)
    return jnp.where(lane % HD < HD // 2, ahead, behind)


def slot_of(block, z, length):
    return pl.multiple_of(((block - z + 4) % 4) * length, 16)


def causal_width(block, length, total):
    return min(total, -(-((block + 1) * length) // 128) * 128)


def masked_scores(q, k, start, first_row):
    s = mm(q, k, ((1,), (1,)))
    col = lax.broadcasted_iota(jnp.int32, s.shape, 1)
    row = lax.broadcasted_iota(jnp.int32, s.shape, 0) + first_row
    return jnp.where((col <= row) & (col >= start), s, MASKED)


def attn_forward_kernel(meta, own, oth, start, cos, sin, att_own, att_oth, rot, lse, nat):
    y, z = meta[0], meta[1]
    total = rot.shape[0]
    half = total // 2
    length = half // 4
    for src, base in ((own, y * half), (oth, (1 - y) * half)):
        for b in range(4):
            at = pl.ds(pl.multiple_of(base + b * length, 16), length)
            rows = src[pl.ds(slot_of(b, z, length), length), :].astype(BF)
            c, s = cos[at, :], sin[at, :]
            for part in range(PW // 128):
                u = rows[:, part * 128 : (part + 1) * 128].astype(F32)
                turned = u * c + pick_turn(u) * s
                if part == PW // 128 - 1:
                    lane = lax.broadcasted_iota(jnp.int32, u.shape, 1)
                    turned = jnp.where(lane < HD, turned, u)
                rot[at, part * 128 : (part + 1) * 128] = turned.astype(BF).astype(F32)
    for b in range(8):
        at = slice(b * length, (b + 1) * length)
        width = causal_width(b, length, total)
        k = rot[:width, QW : QW + HD].astype(BF)
        v = rot[:width, QW + HD :].astype(BF)
        heads = []
        for h in range(GROUP):
            q = (rot[at, h * HD : (h + 1) * HD] * HD**-0.5).astype(BF)
            s = masked_scores(q, k, start[at, :], b * length)
            top = jnp.max(s, axis=1, keepdims=True)
            p = jnp.exp(s - top)
            norm = jnp.sum(p, axis=1, keepdims=True)
            lse[at, h : h + 1] = top + jnp.log(norm)
            p = (p * (1.0 / norm)).astype(BF)
            heads.append(mm(p, v, ((1,), (0,))))
        nat[at, :] = jnp.concatenate(heads, axis=1)
    for dst, base in ((att_own, y * half), (att_oth, (1 - y) * half)):
        for b in range(4):
            at = pl.ds(pl.multiple_of(base + b * length, 16), length)
            dst[pl.ds(slot_of(b, z, length), length), :] = nat[at, :]


def attn_backward_kernel(
    meta, rot, lse, own, oth, start, cos, sin, d_own, d_oth, nat, d_nat, dk, dv
):
    y, z = meta[0], meta[1]
    total = rot.shape[0]
    half = total // 2
    length = half // 4
    for src, base in ((own, y * half), (oth, (1 - y) * half)):
        for b in range(4):
            at = pl.ds(pl.multiple_of(base + b * length, 16), length)
            nat[at, :] = src[pl.ds(slot_of(b, z, length), length), :]
    dk[...] = jnp.zeros_like(dk)
    dv[...] = jnp.zeros_like(dv)
    for b in range(8):
        at = slice(b * length, (b + 1) * length)
        width = causal_width(b, length, total)
        k = rot[:width, QW : QW + HD].astype(BF)
        v = rot[:width, QW + HD :].astype(BF)
        d_heads = []
        for h in range(GROUP):
            q = (rot[at, h * HD : (h + 1) * HD] * HD**-0.5).astype(BF)
            g = nat[at, h * HD : (h + 1) * HD].astype(BF)
            p = jnp.exp(masked_scores(q, k, start[at, :], b * length) - lse[at, h : h + 1])
            dp = mm(g, v, ((1,), (1,)))
            delta = jnp.sum(p * dp, axis=1, keepdims=True)
            ds = (p * (dp - delta)).astype(BF)
            d_heads.append(mm(ds, k, ((1,), (0,))) * HD**-0.5)
            dk[:width, :] += mm(ds, q, ((0,), (0,)))
            dv[:width, :] += mm(p.astype(BF), g, ((0,), (0,)))
        d_q = jnp.concatenate(d_heads, axis=1)
        for part in range(QW // 128):
            u = d_q[:, part * 128 : (part + 1) * 128]
            u = u * cos[at, :] - pick_turn(u) * sin[at, :]
            d_nat[at, part * 128 : (part + 1) * 128] = u
    for b in range(8):
        at = slice(b * length, (b + 1) * length)
        u = jnp.concatenate([dk[at, :], dv[at, :]], axis=1)
        turned = u * cos[at, :] - pick_turn(u) * sin[at, :]
        lane = lax.broadcasted_iota(jnp.int32, u.shape, 1)
        d_nat[at, QW:] = jnp.where(lane < HD, turned, u)
    for dst, base in ((d_own, y * half), (d_oth, (1 - y) * half)):
        for b in range(4):
            at = pl.ds(pl.multiple_of(base + b * length, 16), length)
            dst[pl.ds(slot_of(b, z, length), length), :] = d_nat[at, :]


VMEM = pl.BlockSpec(memory_space=pltpu.VMEM)
SMEM = pl.BlockSpec(memory_space=pltpu.SMEM)
ATTN_PARAMS = dict(vmem_limit_bytes=24 * 1024 * 1024)


def attn_forward(meta, own, oth, start, cos, sin):
    half = own.shape[0]
    return pl.pallas_call(
        attn_forward_kernel,
        out_shape=(
            jax.ShapeDtypeStruct((half, QW), F32),
            jax.ShapeDtypeStruct((half, QW), F32),
            jax.ShapeDtypeStruct((2 * half, PW), F32),
            jax.ShapeDtypeStruct((2 * half, GROUP), F32),
        ),
        in_specs=[SMEM] + [VMEM] * 5,
        out_specs=[VMEM] * 4,
        scratch_shapes=[pltpu.VMEM((2 * half, QW), F32)],
        compiler_params=pltpu.CompilerParams(**ATTN_PARAMS),
        cost_estimate=pl.CostEstimate(
            flops=half * half * QW, bytes_accessed=half * PW, transcendentals=0
        ),
        name="attend_forward",
    )(meta, own, oth, start, cos, sin)


def attn_backward(meta, rot, lse, own, oth, start, cos, sin):
    half = own.shape[0]
    return pl.pallas_call(
        attn_backward_kernel,
        out_shape=(
            jax.ShapeDtypeStruct((half, PW), F32),
            jax.ShapeDtypeStruct((half, PW), F32),
        ),
        in_specs=[SMEM] + [VMEM] * 7,
        out_specs=[VMEM] * 2,
        scratch_shapes=[
            pltpu.VMEM((2 * half, QW), F32),
            pltpu.VMEM((2 * half, PW), F32),
            pltpu.VMEM((2 * half, HD), F32),
            pltpu.VMEM((2 * half, HD), F32),
        ],
        compiler_params=pltpu.CompilerParams(**ATTN_PARAMS),
        cost_estimate=pl.CostEstimate(
            flops=half * half * QW, bytes_accessed=half * PW, transcendentals=0
        ),
        name="attend_backward",
    )(meta, rot, lse, own, oth, start, cos, sin)


def positions_of(seg_row):
    index_row = jnp.arange(seg_row.shape[0], dtype=jnp.int32)
    changed = jnp.concatenate([jnp.ones((1,), bool), seg_row[1:] != seg_row[:-1]])
    starts = lax.cummax(jnp.where(changed, index_row, 0), axis=0)
    return index_row - starts, starts


def rope_tables(positions):
    freq_index = jnp.arange(HD // 2, dtype=F32)
    inverse = THETA ** (-2.0 * freq_index / HD)
    angles = positions.astype(F32)[:, None] * inverse[None, :]
    cosines = jnp.cos(angles)
    sines = jnp.sin(angles)
    return (
        jnp.concatenate([cosines] * 4, axis=-1),
        jnp.concatenate([-sines, sines] * 2, axis=-1),
    )


def rms_scale(values):
    return lax.rsqrt(jnp.mean(values * values, axis=-1, keepdims=True) + EPS)


def norm_backward(grad_normed, normalized, scales, gain):
    rescaled = grad_normed * gain
    grad_input = scales * (
        rescaled - normalized * jnp.mean(rescaled * normalized, axis=-1, keepdims=True)
    )
    return grad_input


def shards(
    count,
    tokens,
    cotangent,
    segments,
    first_gain,
    second_gain,
    query_weight,
    key_weight,
    value_weight,
    output_weight,
    gate_weight,
    up_matrix,
    down_weight,
):
    s = lax.axis_index("shard")
    y = lax.axis_index("context")
    z = lax.axis_index("tensor")
    order = xor_order(count)
    deep = first_gain.shape[0]
    width = deep * count

    def to_xor(rows):
        return jnp.concatenate(
            [lax.dynamic_slice_in_dim(rows, (s ^ o) * deep, deep, axis=1) for o in order], axis=1
        )

    inverse_order = [order.index(o) for o in range(count)]

    def from_xor(rows):
        slots = jnp.array(inverse_order, jnp.int32)
        return jnp.concatenate(
            [
                lax.dynamic_slice_in_dim(rows, slots[s ^ b] * deep, deep, axis=1)
                for b in range(count)
            ],
            axis=1,
        )

    def swap(halves):
        middle = halves.shape[1] // 2
        return jnp.concatenate([halves[:, middle:], halves[:, :middle]], axis=1)

    def own_first(halves):
        return jnp.where(y == 0, halves, swap(halves))

    meta = jnp.stack([y, z]).astype(jnp.int32)
    positions, starts = positions_of(segments[0])
    start_col = starts[:, None]
    cos, sin = rope_tables(positions)

    bits = shard_bits(count)
    line = Order()

    def fetch(piece, axis=0):
        return [piece, xor_send(piece, bits[0], count)]

    def fetch_end(blocks, axis=0):
        for bit in bits[1:]:
            if count > 4:
                blocks = [jnp.concatenate(blocks, axis=axis)]
            blocks = blocks + [xor_send(b, bit, count) for b in blocks]
        return jnp.concatenate(blocks, axis=axis)

    pack = own_first(
        jnp.concatenate(
            [
                piece[:, part * piece.shape[1] // 2 : (part + 1) * piece.shape[1] // 2]
                for part in range(2)
                for piece in (query_weight, key_weight, value_weight)
            ],
            axis=1,
        )
    )
    out_piece = own_first(output_weight)

    rows = to_xor(tokens[0])
    near = gather_rows_start(rows)
    pack_blocks = fetch(pack)
    gains = jnp.stack([first_gain.astype(F32), second_gain.astype(F32)])
    gains = fetch_end(fetch(gains, 1), 1)
    gain_one, gain_two = gains[:1], gains[1:]
    cot = to_xor(cotangent[0])

    pack_blocks = line.wait(pack_blocks)
    out_blocks = fetch(line.after(out_piece))
    w_pack = fetch_end(pack_blocks)
    near = line.wait(near)
    far = gather_rows_next(near)
    out_blocks = line.wait(out_blocks)
    gate_blocks = fetch(line.after(gate_weight))
    w_out = fetch_end(out_blocks)
    far = line.wait(far)
    rows_all = gather_rows_end(rows, near, far)

    rows_f = rows.astype(F32)
    scale_one = rms_scale(rows_f)
    all_f = rows_all.astype(F32)
    hat_all = all_f * rms_scale(all_f)
    normed_all = (hat_all * gain_one).astype(BF)
    proj = line.wait(mm(normed_all, w_pack, ((1,), (0,)), BF))
    proj_own = proj[:, :PW]
    proj_oth = flip(proj[:, PW:])
    cot_near = gather_rows_start(line.after(cot))
    proj_oth = line.wait(proj_oth)
    att_own, att_oth, rot, lse = attn_forward(
        meta, proj_own.astype(F32), proj_oth.astype(F32), start_col, cos, sin
    )
    att_oth = flip(line.wait(att_oth.astype(BF)))
    cot_near = line.wait(cot_near)
    gate_blocks = line.wait(gate_blocks)
    up_blocks = fetch(line.after(up_matrix))
    w_gate = fetch_end(gate_blocks)
    att_oth = line.wait(att_oth)
    context = jnp.concatenate([att_own.astype(BF), att_oth], axis=1)
    attn_terms = line.wait(mm(context, w_out, ((1,), (1,)), BF))
    far = sum_rows_start(attn_terms)
    far = line.wait(far)
    near = sum_rows_next(attn_terms, far)
    up_blocks = line.wait(up_blocks)
    down_blocks = fetch(line.after(down_weight))
    w_up = fetch_end(up_blocks)
    near = line.wait(near)
    attn = sum_rows_end(attn_terms, near)

    hidden_one = rows_f + attn
    scale_two = rms_scale(hidden_one)
    hat_two = hidden_one * scale_two
    normed_two = line.wait((hat_two * gain_two).astype(BF))
    near = line.wait(gather_rows_start(normed_two))
    far = line.wait(gather_rows_next(near))
    cot_far = gather_rows_next(line.after(cot_near))
    normed_two_all = gather_rows_end(normed_two, near, far)
    gate = mm(normed_two_all, w_gate, ((1,), (0,)))
    down_blocks, gate = line.wait((down_blocks, gate))
    w_down = fetch_end(down_blocks)
    up = mm(normed_two_all, w_up, ((1,), (0,)))
    sig = jax.nn.sigmoid(gate)
    silu = gate * sig
    hidden, cot_far = line.wait(((silu * up).astype(BF), cot_far))
    cot_all = gather_rows_end(cot, cot_near, cot_far)

    def grad_start(left, right):
        half = width // 2
        term = mm(left[:, half:], right, ((0,), (0,)), BF)
        sent = xor_send(term, bits[-1], count)
        return mm(left[:, :half], right, ((0,), (0,)), BF), sent

    def grad_next(kept, sent, pieces):
        kept = line.wait(add_bf(kept, sent))
        if len(bits) != 2:
            return [(reduce_rest(kept, bits[:-1][::-1], count), None)]
        size = kept.shape[0] // 2 // pieces
        return [
            (
                kept[i * size : (i + 1) * size],
                xor_send(kept[(pieces + i) * size : (pieces + i + 1) * size], bits[-2], count),
            )
            for i in range(pieces)
        ]

    def grad_end(halves, at):
        kept, sent = halves[min(at, len(halves) - 1)]
        if sent is not None:
            kept = line.wait(add_bf(kept, line.wait(sent)))
        elif at:
            return None
        return kept, flip(kept)

    def both(pairs):
        return jnp.concatenate([p[0].astype(F32) + p[1].astype(F32) for p in pairs if p], axis=0)

    down_pair = grad_start(cot_all, hidden)
    down_half = grad_next(*down_pair, 2)
    grad_hidden = mm(line.after(cot_all), w_down, ((1,), (0,)))
    grad_gate = (grad_hidden * up * sig * (1.0 + gate * (1.0 - sig))).astype(BF)
    grad_up = (grad_hidden * silu).astype(BF)
    grad_gate, grad_up = line.wait((grad_gate, grad_up))
    mid_terms = mm(grad_gate, w_gate, ((1,), (1,))) + mm(grad_up, w_up, ((1,), (1,)))
    mid_terms = line.wait(mid_terms.astype(BF))
    far = sum_rows_start(mid_terms)
    far = line.wait(far)
    near = sum_rows_next(mid_terms, far)
    normed_left, grad_gate = line.after((normed_two_all, grad_gate))
    gate_pair = grad_start(normed_left, grad_gate)
    down_a = grad_end(down_half, 0)
    gate_half = grad_next(*gate_pair, 2)
    near = line.wait(near)
    normed_two_grad = sum_rows_end(mid_terms, near)

    resid = cot.astype(F32) + norm_backward(normed_two_grad, hat_two, scale_two, gain_two)
    gain_two_part = jnp.sum(normed_two_grad * hat_two, axis=0)

    resid_low = line.wait(resid.astype(BF))
    near = gather_rows_start(resid_low)
    normed_left, grad_up = line.after((normed_two_all, grad_up))
    up_pair = grad_start(normed_left, grad_up)
    down_b = grad_end(down_half, 1)
    near = line.wait(near)
    far = line.wait(gather_rows_next(near))
    resid_all = gather_rows_end(resid_low, near, far)
    grad_context = line.wait(mm(resid_all, w_out, ((1,), (0,)), BF))
    g_own = grad_context[:, :QW]
    g_oth = flip(grad_context[:, QW:])
    ffn_terms = line.wait(mm(line.after(hidden), w_down, ((1,), (1,)), BF))
    ffn_far = sum_rows_start(ffn_terms)
    gate_a = grad_end(gate_half, 0)
    up_half = grad_next(*up_pair, 2)
    g_oth = line.wait(g_oth)
    gate_b = grad_end(gate_half, 1)
    ffn_far = line.wait(ffn_far)
    ffn_near = sum_rows_next(ffn_terms, ffn_far)
    d_own, d_oth = attn_backward(
        meta, rot, lse, g_own.astype(F32), g_oth.astype(F32), start_col, cos, sin
    )
    down_a, down_b, gate_a, gate_b, ffn_near, up_half[0], d_oth = line.wait(
        (down_a, down_b, gate_a, gate_b, ffn_near, up_half[0], d_oth.astype(BF))
    )
    d_oth = flip(d_oth)
    up_a = grad_end(up_half, 0)
    layer_output = (hidden_one + sum_rows_end(ffn_terms, ffn_near)).astype(BF)
    layer_output = line.wait(layer_output)
    d_oth = line.wait(d_oth)
    d_pack = jnp.concatenate([d_own.astype(BF), d_oth], axis=1)
    one_terms = mm(d_pack, w_pack, ((1,), (1,)))
    gain_one_part = jnp.sum(one_terms * hat_all, axis=0)
    one_low, part = line.wait((one_terms.astype(BF), jnp.stack([gain_one_part, gain_two_part])))
    far = sum_rows_start(one_low)
    part_terms = [part] + [shift(part, -step) for step in (1, 2, 3)]
    normed_left, d_pack, resid_left, context = line.after((normed_all, d_pack, resid_all, context))
    pack_pair = grad_start(normed_left, d_pack)
    far = line.wait(far)
    near = sum_rows_next(one_low, far)
    out_half = grad_next(*grad_start(resid_left, context), 1)
    up_b = grad_end(up_half, 1)
    out_full = grad_end(out_half, 0)
    pack_half = grad_next(*pack_pair, 1)

    down_total = both(line.wait([down_a, down_b]))
    pack_full = grad_end(pack_half, 0)
    gate_total = both([gate_a, gate_b])

    near = line.wait(near)
    normed_one_grad = sum_rows_end(one_low, near)
    back = norm_backward(normed_one_grad, rows_f * scale_one, scale_one, gain_one)
    tokens_grad = (resid + back).astype(BF)

    def both_swapped(pair):
        return own_first(pair[0].astype(F32) + swap(pair[1]).astype(F32))

    up_total = both(line.wait([up_a, up_b]))

    part_terms = jnp.stack(part_terms + part_terms)
    part = jnp.sum(lax.dynamic_slice_in_dim(part_terms, (4 - z) % 4, 4, axis=0), axis=0)
    size = width
    for bit in bits[::-1]:
        size = size // 2
        part = part[:, :size] + xor_send(part[:, size:], bit, count)
    gain_total = part + flip(part)
    out_total = both_swapped(line.wait(out_full))
    pack_total = both_swapped(pack_full)
    query_parts, key_parts, value_parts = (
        jnp.concatenate([pack_total[:, at : at + size], pack_total[:, PW + at : PW + at + size]], 1)
        for at, size in ((0, QW), (QW, HD), (QW + HD, HD))
    )
    return (
        from_xor(layer_output)[None],
        from_xor(tokens_grad)[None],
        gain_total[0] + line.mark,
        gain_total[1],
        query_parts,
        key_parts,
        value_parts,
        out_total,
        gate_total,
        up_total,
        down_total,
    )


def solution(mesh):
    return jax.shard_map(
        functools.partial(shards, mesh.shape["shard"]),
        mesh=mesh,
        in_specs=(
            P("shard", ("context", "tensor"), None),
            P("shard", ("context", "tensor"), None),
            P("shard", None),
            P("shard"),
            P("shard"),
            P("shard", "tensor"),
            P("shard", "tensor"),
            P("shard", "tensor"),
            P("shard", "tensor"),
            P("shard", "tensor"),
            P("shard", "tensor"),
            P("shard", "tensor"),
        ),
        out_specs=(
            P("shard", ("context", "tensor"), None),
            P("shard", ("context", "tensor"), None),
            P("shard"),
            P("shard"),
            P("shard", "tensor"),
            P("shard", "tensor"),
            P("shard", "tensor"),
            P("shard", "tensor"),
            P("shard", "tensor"),
            P("shard", "tensor"),
            P("shard", "tensor"),
        ),
        check_vma=False,
    )
```
